32 devices in a mesh: row: 4 (over z), col: 8 (over y, x, core).
Axes of the slice: x: 2, y: 2, z: 4, core: 2. Of those that a mesh axis runs over, the one named last changes fastest.
Arguments:
- sample: float32 [2, 2048, 4096], P(None, 'row', 'col'), may hold values from -6 to 6
- probe_modes: float32 [2, 2, 256, 256], replicated, may hold values from -6 to 6
- amplitude: bfloat16 [4, 8, 16, 256, 256], P('row', 'col'), may hold values from 0.5 to 3
- offsets: int32 [4, 8, 16, 2], P('row', 'col'), may hold values from 0 to 511, as said below
- counts: int32 [4, 8], P('row', 'col'), may hold values from 1 to 16, as said below
Outputs:
- new_sample: float32 [2, 2048, 4096], P(None, 'row', 'col')
- new_probe: float32 [2, 2, 256, 256], replicated
The draws below stay inside these ranges and needn't reach their ends.
Inputs may be any that keep to these rules, and one draw needn't show every extreme that they name: `counts`: every tile has at least one live slot; some tile has exactly 16 live slots and some exactly 1. offsets[..., 0] is a row below 512, offsets[..., 1] a column below 512.
All inputs are finite; a program needn't handle non-finite values.
Results may differ from the reference program's by a relative error of at most 0.0029.
Values may be sent and summed in bfloat16 or wider, within the bound.
A program may use at most 128 MiB of HBM per device.

```python
import math
import jax
import jax.numpy as jnp
from jax import lax

FRAME = 256
MODES = 2
TILE_R = 512
TILE_C = 512
CAP = 16
TOTAL_R = 2048
TOTAL_C = 4096
N_ROW = 4
N_COL = 8


def draw_counts(key, part):
    first_key, second_key, third_key = jax.random.split(jax.random.fold_in(key, 11), 3)
    first = jax.random.randint(first_key, (N_ROW, N_COL), 1, CAP + 1)
    second = jax.random.randint(second_key, (N_ROW, N_COL), 1, CAP + 1)
    mixed = (first * second + CAP - 1) // CAP
    chosen = jax.random.randint(third_key, (), 0, N_ROW * N_COL)
    flat_index = jnp.arange(N_ROW * N_COL, dtype=jnp.int32).reshape(N_ROW, N_COL)
    mixed = jnp.where(flat_index == chosen, CAP, mixed)
    mixed = jnp.where(flat_index == (chosen + 1) % (N_ROW * N_COL), 1, mixed)
    return mixed.astype(jnp.int32)


def draw_offsets(key, part):
    row_key, col_key = jax.random.split(jax.random.fold_in(key, 23), 2)
    rows = jax.random.randint(row_key, (N_ROW, N_COL, CAP), 0, TILE_R)
    cols = jax.random.randint(col_key, (N_ROW, N_COL, CAP), 0, TILE_C)
    flat_index = jnp.arange(N_ROW * N_COL * CAP, dtype=jnp.int32).reshape(N_ROW, N_COL, CAP)
    rows = jnp.where(flat_index == 0, TILE_R - 1, rows)
    cols = jnp.where(flat_index == 0, TILE_C - 1, cols)
    last_first = (N_ROW * N_COL - 1) * CAP
    rows = jnp.where(flat_index == last_first, 0, rows)
    cols = jnp.where(flat_index == last_first, 0, cols)
    return jnp.stack([rows, cols], axis=-1).astype(jnp.int32)


def block_scale(stream_key, shape, shards, least, top_value):
    gain, own = 1.0, jax.random.fold_in(stream_key, 6)
    for position, parts in shards:
        heights = jnp.exp(jax.random.uniform(jax.random.fold_in(own, position), (parts,), jnp.float32, least / len(shards), top_value / len(shards)))
        gain = gain * jnp.repeat(heights, shape[position] // parts).reshape([-1 if axis == position else 1 for axis in range(len(shape))])
    return gain


def centred(stream_key, extent, spread, most, shards=(), held_as=jnp.bfloat16):
    entries = jax.random.normal(stream_key, extent, jnp.float32) * spread
    if len(shards) > 0:
        entries = block_scale(stream_key, extent, shards, -0.22, 0.18) * entries
    return jnp.clip(entries, min=-most, max=most).astype(held_as)


def setup_inputs(seed: int = 0) -> dict:
    key_list = jax.random.split(jax.random.key(seed), 6)
    return {
        "sample": centred(key_list[0], (2, TOTAL_R, TOTAL_C), 1.0, 6.0, ((1, 4), (2, 8)), jnp.float32),
        "probe_modes": centred(key_list[1], (MODES, 2, FRAME, FRAME), 1.0, 6.0, (), jnp.float32),
        "amplitude": jnp.clip(0.5 + 2.5 * jax.random.uniform(key_list[2], (N_ROW, N_COL, CAP, FRAME, FRAME), jnp.float32) ** block_scale(key_list[2], (N_ROW, N_COL, CAP, FRAME, FRAME), ((0, 4), (1, 8)), -0.2, 0.2), 0.5, 3.0).astype(jnp.bfloat16),
        "offsets": draw_offsets(jax.random.fold_in(key_list[5], 71), 0),
        "counts": draw_counts(jax.random.fold_in(key_list[5], 71), 0),
    }


def dft_tables(frame):
    index = jnp.arange(frame, dtype=jnp.int32)
    product = index[:, None] * index[None, :] % frame
    angle = 2.0 * math.pi / frame * product.astype(jnp.float32)
    scale = 1.0 / math.sqrt(frame)
    return ((jnp.cos(angle) * scale).astype(jnp.bfloat16), (-jnp.sin(angle) * scale).astype(jnp.bfloat16))

def apply_left(w_real, w_imag, x_real, x_imag):

    def product_of(table, field):
        return jnp.einsum('jk,mkl->mjl', table.astype(jnp.float32), field.astype(jnp.float32))
    return (product_of(w_real, x_real) - product_of(w_imag, x_imag), product_of(w_real, x_imag) + product_of(w_imag, x_real))

def apply_right(x_real, x_imag, w_real, w_imag):

    def product_of(field, table):
        return jnp.einsum('mjk,kl->mjl', field.astype(jnp.float32), table.astype(jnp.float32))
    return (product_of(x_real, w_real) - product_of(x_imag, w_imag), product_of(x_real, w_imag) + product_of(x_imag, w_real))

def make_wave(patch, probe_modes):
    probe_real = probe_modes[:, 0]
    probe_imag = probe_modes[:, 1]
    wave_real = (probe_real * patch[0] - probe_imag * patch[1]).astype(jnp.bfloat16)
    wave_imag = (probe_real * patch[1] + probe_imag * patch[0]).astype(jnp.bfloat16)
    return (wave_real, wave_imag)

def wave_gradient(wave_real, wave_imag, measured, w_real, w_imag):
    half_real, half_imag = apply_left(w_real, w_imag, wave_real, wave_imag)
    far_real, far_imag = apply_right(half_real.astype(jnp.bfloat16), half_imag.astype(jnp.bfloat16), w_real, w_imag)
    intensity = lax.optimization_barrier(jnp.sum(far_real * far_real + far_imag * far_imag, axis=0))
    factor = 1.0 - measured.astype(jnp.float32) / jnp.maximum(jnp.sqrt(intensity), 0.25)
    corr_real = (far_real * factor).astype(jnp.bfloat16)
    corr_imag = (far_imag * factor).astype(jnp.bfloat16)
    conj_imag = -w_imag
    back_real, back_imag = apply_left(w_real, conj_imag, corr_real, corr_imag)
    grad_real, grad_imag = apply_right(back_real.astype(jnp.bfloat16), back_imag.astype(jnp.bfloat16), w_real, conj_imag)
    return (grad_real.astype(jnp.bfloat16), grad_imag.astype(jnp.bfloat16))

def add_terms(state, patch, row_at, col_at, grad_real, grad_imag, probe_modes):
    object_grad, probe_grad = state
    g_real = grad_real.astype(jnp.float32)
    g_imag = grad_imag.astype(jnp.float32)
    probe_real = probe_modes[:, 0]
    probe_imag = probe_modes[:, 1]
    term_real = lax.optimization_barrier(jnp.sum(probe_real * g_real + probe_imag * g_imag, axis=0))
    term_imag = lax.optimization_barrier(jnp.sum(probe_real * g_imag - probe_imag * g_real, axis=0))
    frame = patch.shape[-1]
    anchor = (jnp.int32(0), row_at, col_at)
    current = lax.dynamic_slice(object_grad, anchor, (2, frame, frame))
    object_grad = lax.dynamic_update_slice(object_grad, current + jnp.stack([term_real, term_imag]), anchor)
    probe_term_real = patch[0] * g_real + patch[1] * g_imag
    probe_term_imag = patch[0] * g_imag - patch[1] * g_real
    probe_grad = probe_grad + jnp.stack([probe_term_real, probe_term_imag], axis=1)
    return (object_grad, probe_grad)

def reference(sample, probe_modes, amplitude, offsets, counts):
    w_real, w_imag = dft_tables(FRAME)
    padded = jnp.pad(sample, ((0, 0), (0, FRAME), (0, FRAME)))
    initial = (jnp.zeros(padded.shape, jnp.float32), jnp.zeros(probe_modes.shape, jnp.float32))

    def visit(state, flat):
        tile_row = flat // (N_COL * CAP)
        tile_col = flat // CAP % N_COL
        slot = flat % CAP
        row_at = (tile_row * TILE_R + offsets[tile_row, tile_col, slot, 0]).astype(jnp.int32)
        col_at = (tile_col * TILE_C + offsets[tile_row, tile_col, slot, 1]).astype(jnp.int32)

        def live(carried):
            patch = lax.dynamic_slice(padded, (jnp.int32(0), row_at, col_at), (2, FRAME, FRAME))
            wave_real, wave_imag = make_wave(patch, probe_modes)
            grad_real, grad_imag = wave_gradient(wave_real, wave_imag, amplitude[tile_row, tile_col, slot], w_real, w_imag)
            return add_terms(carried, patch, row_at, col_at, grad_real, grad_imag, probe_modes)

        def unchanged(carried):
            return carried
        return (lax.cond(slot < counts[tile_row, tile_col], live, unchanged, state), None)
    (object_grad, probe_grad), _ = lax.scan(visit, initial, jnp.arange(N_ROW * N_COL * CAP, dtype=jnp.int32))
    object_grad = object_grad[:, :TOTAL_R, :TOTAL_C]
    probe_power = lax.optimization_barrier(jnp.sum(probe_modes[:, 0] ** 2 + probe_modes[:, 1] ** 2, axis=0))
    peak = jnp.max(probe_power) + 1e-06
    new_sample = sample - object_grad / peak
    new_probe = probe_modes - probe_grad / math.sqrt(N_ROW * N_COL * CAP)
    return (new_sample, new_probe)
```

```python
import math

import jax
import jax.numpy as jnp
import ml_dtypes
import numpy as np
from jax import lax
from jax.experimental import pallas as pl
from jax.experimental.pallas import tpu as pltpu
from jax.sharding import PartitionSpec as P

LANES = 128
CHUNK = 16


def shifted(block, axes, distances):
    sizes = [lax.axis_size(a) for a in axes]
    route = []
    for flat in range(math.prod(sizes)):
        at = np.unravel_index(flat, sizes)
        to = [int(i) + d for i, d in zip(at, distances)]
        if all(0 <= i < n for i, n in zip(to, sizes)):
            route.append((flat, int(np.ravel_multi_index(to, sizes))))
    return lax.ppermute(block, axes, route)


def tables(frame):
    index = np.arange(frame)
    angle = 2.0 * math.pi / frame * ((index[:, None] * index[None, :]) % frame)
    scale = 1.0 / math.sqrt(frame)
    w_real, w_imag = np.cos(angle) * scale, -np.sin(angle) * scale

    def block(first):
        real, imag = w_real[first::2, : frame // 2], w_imag[first::2, : frame // 2]
        return np.block([[real, -imag], [imag, real]])

    even, odd = block(0), block(1)
    order = np.concatenate([index[0::2], index[1::2]])
    pick = np.eye(frame)[order]
    stack = np.stack([even, odd, even.T, odd.T, pick, pick.T])
    return stack.astype(np.float32).astype(ml_dtypes.bfloat16)


def gradient_kernel(
    offsets, counts, table, sample, right, below, corner, probe, amplitude,
    main_out, right_out, below_out, corner_out, probe_out,
    ext, acc, patch, xs, ys, zs, gs,
):
    rows, cols = sample.shape[1:]
    frame = probe.shape[-1]
    half = frame // 2
    own = cols // LANES
    wide = ext.shape[1]
    f32, bf16 = jnp.float32, jnp.bfloat16

    for c in range(2):
        for j in range(own):
            at = slice(j * LANES, (j + 1) * LANES)
            ext[c, j, :rows, :] = sample[c, :, at]
            ext[c, j, rows:, :] = below[c, :, at].astype(f32)
        for j in range(own, wide):
            at = slice((j - own) * LANES, (j - own + 1) * LANES)
            ext[c, j, :rows, :] = right[c, :, at].astype(f32)
            ext[c, j, rows:, :] = corner[c, :, at].astype(f32)
    acc[...] = jnp.zeros_like(acc)
    probe_out[...] = jnp.zeros_like(probe_out)

    def dot(a, b):
        return jnp.dot(a, b, preferred_element_type=f32)

    def visit(slot, carry):
        row_at = offsets[2 * slot]
        col_at = offsets[2 * slot + 1]
        panel = col_at // LANES
        lane_at = col_at % LANES
        back_by = lax.rem(LANES - lane_at, LANES)
        lane = lax.broadcasted_iota(jnp.int32, (CHUNK, LANES), 1)
        inside = lane < LANES - lane_at
        after = lane >= lane_at

        measured = dot(table[4], amplitude[slot]).astype(bf16)
        measured = dot(measured, table[5])

        def window(c, t):
            parts = [
                pltpu.roll(ext[c, panel + j, pl.ds(row_at + t, CHUNK), :], back_by, 1)
                for j in range(3)
            ]
            return [jnp.where(inside, parts[j], parts[j + 1]) for j in range(2)]

        for t in range(0, half, CHUNK):
            waves = []
            for h in range(2):
                u = h * half + t
                o_real, o_imag = window(0, u), window(1, u)
                wave = {}
                for j in range(2):
                    at = slice(j * LANES, (j + 1) * LANES)
                    patch[0, u : u + CHUNK, at] = o_real[j]
                    patch[1, u : u + CHUNK, at] = o_imag[j]
                    for m in range(2):
                        p_real = probe[m, 0, u : u + CHUNK, at]
                        p_imag = probe[m, 1, u : u + CHUNK, at]
                        wave[m, j, 0] = p_real * o_real[j] - p_imag * o_imag[j]
                        wave[m, j, 1] = p_real * o_imag[j] + p_imag * o_real[j]
                waves.append(wave)
            for m in range(2):
                for j in range(2):
                    at = slice(m * frame + j * LANES, m * frame + (j + 1) * LANES)
                    for c in range(2):
                        low, high = waves[0][m, j, c], waves[1][m, j, c]
                        to = slice(c * half + t, c * half + t + CHUNK)
                        xs[0, to, at] = (low + high).astype(bf16)
                        xs[1, to, at] = (low - high).astype(bf16)

        for p in range(2):
            product = dot(table[p], xs[p])
            for m in range(2):
                to = slice((2 * p + m) * half, (2 * p + m + 1) * half)
                for c in range(2):
                    value = product[c * half : (c + 1) * half, m * frame : (m + 1) * frame]
                    low, high = value[:, :half], value[:, half:]
                    at = slice(c * half, (c + 1) * half)
                    ys[0, to, at] = (low + high).astype(bf16)
                    ys[1, to, at] = (low - high).astype(bf16)

        for q in range(2):
            far = dot(ys[q], table[2 + q])
            for p in range(2):
                rows_of = [slice((2 * p + m) * half, (2 * p + m + 1) * half) for m in range(2)]
                fields = [[far[r, :half], far[r, half:]] for r in rows_of]
                intensity = sum(f[0] * f[0] + f[1] * f[1] for f in fields)
                level = measured[p * half : (p + 1) * half, q * half : (q + 1) * half]
                factor = 1.0 - level * lax.rsqrt(jnp.maximum(intensity, 0.0625))
                for m in range(2):
                    at = slice(m * frame + q * half, m * frame + (q + 1) * half)
                    for c in range(2):
                        zs[p, c * half : (c + 1) * half, at] = (fields[m][c] * factor).astype(bf16)

        from_even = dot(table[2], zs[0])
        from_odd = dot(table[3], zs[1])
        for h, back in enumerate((from_even + from_odd, from_even - from_odd)):
            for m in range(2):
                to = slice((2 * h + m) * half, (2 * h + m + 1) * half)
                for q in range(2):
                    at = slice(m * frame + q * half, m * frame + (q + 1) * half)
                    for c in range(2):
                        gs[q, to, c * half : (c + 1) * half] = back[
                            c * half : (c + 1) * half, at
                        ].astype(bf16)

        grad_even = dot(gs[0], table[0])
        grad_odd = dot(gs[1], table[1])
        for t in range(0, frame, CHUNK):
            h, u = divmod(t, half)
            terms = [[None, None], [None, None]]
            for j in range(2):
                at = slice(j * LANES, (j + 1) * LANES)
                here = slice(t, t + CHUNK)
                o_real, o_imag = patch[0, here, at], patch[1, here, at]
                for m in range(2):
                    of = slice((2 * h + m) * half + u, (2 * h + m) * half + u + CHUNK)
                    g = []
                    for c in range(2):
                        e = grad_even[of, c * half : (c + 1) * half]
                        o = grad_odd[of, c * half : (c + 1) * half]
                        g.append(e + o if j == 0 else e - o)
                    p_real, p_imag = probe[m, 0, here, at], probe[m, 1, here, at]
                    add_real = p_real * g[0] + p_imag * g[1]
                    add_imag = p_real * g[1] - p_imag * g[0]
                    terms[0][j] = add_real if m == 0 else terms[0][j] + add_real
                    terms[1][j] = add_imag if m == 0 else terms[1][j] + add_imag
                    probe_out[m, 0, here, at] += o_real * g[0] + o_imag * g[1]
                    probe_out[m, 1, here, at] += o_real * g[1] - o_imag * g[0]
            for c in range(2):
                first = pltpu.roll(terms[c][0], lane_at, 1)
                second = pltpu.roll(terms[c][1], lane_at, 1)
                spread = (
                    jnp.where(after, first, 0.0),
                    jnp.where(after, second, first),
                    jnp.where(after, 0.0, second),
                )
                for j in range(3):
                    acc[c, panel + j, pl.ds(row_at + t, CHUNK), :] += spread[j]
        return carry

    lax.fori_loop(0, counts[0], visit, 0)

    for c in range(2):
        for j in range(own):
            at = slice(j * LANES, (j + 1) * LANES)
            main_out[c, :, at] = acc[c, j, :rows, :]
            below_out[c, :, at] = acc[c, j, rows:, :].astype(bf16)
        for j in range(own, wide):
            at = slice((j - own) * LANES, (j - own + 1) * LANES)
            right_out[c, :, at] = acc[c, j, :rows, :].astype(bf16)
            corner_out[c, :, at] = acc[c, j, rows:, :].astype(bf16)


def shards(sample, probe_modes, amplitude, offsets, counts):
    frame = probe_modes.shape[-1]
    rows, cols = sample.shape[1:]
    slots = amplitude.shape[2]
    f32, bf16 = jnp.float32, jnp.bfloat16
    edge = sample.astype(bf16)
    right = shifted(edge[:, :, :frame], ("row", "col"), (0, -1))
    below = shifted(edge[:, :frame, :], ("row", "col"), (-1, 0))
    corner = shifted(edge[:, :frame, :frame], ("row", "col"), (-1, -1))
    panels = (cols + frame) // LANES
    shape = jax.ShapeDtypeStruct
    vmem = pl.BlockSpec(memory_space=pltpu.VMEM)
    smem = pl.BlockSpec(memory_space=pltpu.SMEM)
    main, right_grad, below_grad, corner_grad, probe_grad = pl.pallas_call(
        gradient_kernel,
        out_shape=(
            shape((2, rows, cols), f32),
            shape((2, rows, frame), bf16),
            shape((2, frame, cols), bf16),
            shape((2, frame, frame), bf16),
            shape(probe_modes.shape, f32),
        ),
        in_specs=[smem, smem] + [vmem] * 7,
        out_specs=(vmem,) * 5,
        scratch_shapes=[
            pltpu.VMEM((2, panels, rows + frame, LANES), f32),
            pltpu.VMEM((2, panels, rows + frame, LANES), f32),
            pltpu.VMEM((2, frame, frame), f32),
            pltpu.VMEM((2, frame, 2 * frame), bf16),
            pltpu.VMEM((2, 2 * frame, frame), bf16),
            pltpu.VMEM((2, frame, 2 * frame), bf16),
            pltpu.VMEM((2, 2 * frame, frame), bf16),
        ],
        compiler_params=pltpu.CompilerParams(vmem_limit_bytes=48 * 1024 * 1024),
    )(
        offsets.reshape(-1), counts.reshape(-1), jnp.asarray(tables(frame)), sample,
        right, below, corner, probe_modes, amplitude.reshape(slots, frame, frame),
    )
    from_left = shifted(right_grad, ("row", "col"), (0, 1))
    from_above = shifted(below_grad, ("row", "col"), (1, 0))
    from_both = shifted(corner_grad, ("row", "col"), (1, 1))
    summed = lax.psum(probe_grad, ("row", "col"))

    def placed(block):
        tall, broad = rows - block.shape[1], cols - block.shape[2]
        return jnp.pad(block.astype(f32), ((0, 0), (0, tall), (0, broad)))

    total = main + placed(from_left) + placed(from_above) + placed(from_both)
    power = jnp.sum(probe_modes[:, 0] ** 2 + probe_modes[:, 1] ** 2, axis=0)
    new_sample = sample - total / (jnp.max(power) + 1e-06)
    devices = lax.axis_size("row") * lax.axis_size("col")
    new_probe = probe_modes - (1.0 / math.sqrt(devices * slots)) * summed
    return (new_sample, new_probe)


def solution(mesh):
    in_specs = (
        P(None, "row", "col"),
        P(),
        P("row", "col", None, None, None),
        P("row", "col", None, None),
        P("row", "col"),
    )
    out_specs = (P(None, "row", "col"), P())
    return jax.shard_map(shards, mesh=mesh, in_specs=in_specs, out_specs=out_specs, check_vma=False)
```

```python
import functools
import math

import jax
import jax.numpy as jnp
import ml_dtypes
import numpy as np
from jax import lax
from jax.experimental import pallas as pl
from jax.experimental.pallas import tpu as pltpu
from jax.sharding import PartitionSpec as P

LANES = 128
CHUNK = 16


def shifted(block, axes, distances):
    sizes = [lax.axis_size(a) for a in axes]
    route = []
    for flat in range(math.prod(sizes)):
        at = np.unravel_index(flat, sizes)
        to = [int(i) + d for i, d in zip(at, distances)]
        if all(0 <= i < n for i, n in zip(to, sizes)):
            route.append((flat, int(np.ravel_multi_index(to, sizes))))
    return lax.ppermute(block, axes, route)


def tables(frame):
    index = np.arange(frame)
    angle = 2.0 * math.pi / frame * ((index[:, None] * index[None, :]) % frame)
    scale = 1.0 / math.sqrt(frame)
    w_real, w_imag = np.cos(angle) * scale, -np.sin(angle) * scale

    def block(first):
        real, imag = w_real[first::2, : frame // 2], w_imag[first::2, : frame // 2]
        return np.block([[real, -imag], [imag, real]])

    even, odd = block(0), block(1)
    order = np.concatenate([index[0::2], index[1::2]])
    pick = np.eye(frame)[order]
    stack = np.stack([even, odd, even.T, odd.T, pick, pick.T])
    return stack.astype(np.float32).astype(ml_dtypes.bfloat16)


def gradient_kernel(
    offsets, counts, table, sample, right, below, corner, probe, amplitude,
    main_out, right_out, below_out, corner_out, probe_out,
    ext, acc, patch, xs, ys, zs, gs,
):
    rows, cols = sample.shape[1:]
    frame = probe.shape[-1]
    half = frame // 2
    own = cols // LANES
    wide = ext.shape[1]
    f32, bf16 = jnp.float32, jnp.bfloat16

    for c in range(2):
        for j in range(own):
            at = slice(j * LANES, (j + 1) * LANES)
            ext[c, j, :rows, :] = sample[c, :, at]
            ext[c, j, rows:, :] = below[c, :, at].astype(f32)
        for j in range(own, wide):
            at = slice((j - own) * LANES, (j - own + 1) * LANES)
            ext[c, j, :rows, :] = right[c, :, at].astype(f32)
            ext[c, j, rows:, :] = corner[c, :, at].astype(f32)
    acc[...] = jnp.zeros_like(acc)
    probe_out[...] = jnp.zeros_like(probe_out)

    def dot(a, b):
        return jnp.dot(a, b, preferred_element_type=f32)

    def visit(slot, carry):
        row_at = offsets[2 * slot]
        col_at = offsets[2 * slot + 1]
        panel = col_at // LANES
        lane_at = col_at % LANES
        back_by = lax.rem(LANES - lane_at, LANES)
        lane = lax.broadcasted_iota(jnp.int32, (CHUNK, LANES), 1)
        inside = lane < LANES - lane_at
        after = lane >= lane_at

        measured = dot(table[4], amplitude[slot]).astype(bf16)
        measured = dot(measured, table[5])

        def window(c, t):
            parts = [
                pltpu.roll(ext[c, panel + j, pl.ds(row_at + t, CHUNK), :], back_by, 1)
                for j in range(3)
            ]
            return [jnp.where(inside, parts[j], parts[j + 1]) for j in range(2)]

        for t in range(0, half, CHUNK):
            waves = []
            for h in range(2):
                u = h * half + t
                o_real, o_imag = window(0, u), window(1, u)
                wave = {}
                for j in range(2):
                    at = slice(j * LANES, (j + 1) * LANES)
                    patch[0, u : u + CHUNK, at] = o_real[j]
                    patch[1, u : u + CHUNK, at] = o_imag[j]
                    for m in range(2):
                        p_real = probe[m, 0, u : u + CHUNK, at]
                        p_imag = probe[m, 1, u : u + CHUNK, at]
                        wave[m, j, 0] = p_real * o_real[j] - p_imag * o_imag[j]
                        wave[m, j, 1] = p_real * o_imag[j] + p_imag * o_real[j]
                waves.append(wave)
            for m in range(2):
                for j in range(2):
                    at = slice(m * frame + j * LANES, m * frame + (j + 1) * LANES)
                    for c in range(2):
                        low, high = waves[0][m, j, c], waves[1][m, j, c]
                        to = slice(c * half + t, c * half + t + CHUNK)
                        xs[0, to, at] = (low + high).astype(bf16)
                        xs[1, to, at] = (low - high).astype(bf16)

        for p in range(2):
            product = dot(table[p], xs[p])
            for m in range(2):
                to = slice((2 * p + m) * half, (2 * p + m + 1) * half)
                for c in range(2):
                    value = product[c * half : (c + 1) * half, m * frame : (m + 1) * frame]
                    low, high = value[:, :half], value[:, half:]
                    at = slice(c * half, (c + 1) * half)
                    ys[0, to, at] = (low + high).astype(bf16)
                    ys[1, to, at] = (low - high).astype(bf16)

        for q in range(2):
            far = dot(ys[q], table[2 + q])
            for p in range(2):
                rows_of = [slice((2 * p + m) * half, (2 * p + m + 1) * half) for m in range(2)]
                fields = [[far[r, :half], far[r, half:]] for r in rows_of]
                intensity = sum(f[0] * f[0] + f[1] * f[1] for f in fields)
                level = measured[p * half : (p + 1) * half, q * half : (q + 1) * half]
                factor = 1.0 - level * lax.rsqrt(jnp.maximum(intensity, 0.0625))
                for m in range(2):
                    at = slice(m * frame + q * half, m * frame + (q + 1) * half)
                    for c in range(2):
                        zs[p, c * half : (c + 1) * half, at] = (fields[m][c] * factor).astype(bf16)

        from_even = dot(table[2], zs[0])
        from_odd = dot(table[3], zs[1])
        for h, back in enumerate((from_even + from_odd, from_even - from_odd)):
            for m in range(2):
                to = slice((2 * h + m) * half, (2 * h + m + 1) * half)
                for q in range(2):
                    at = slice(m * frame + q * half, m * frame + (q + 1) * half)
                    for c in range(2):
                        gs[q, to, c * half : (c + 1) * half] = back[
                            c * half : (c + 1) * half, at
                        ].astype(bf16)

        grad_even = dot(gs[0], table[0])
        grad_odd = dot(gs[1], table[1])
        for t in range(0, frame, CHUNK):
            h, u = divmod(t, half)
            terms = [[None, None], [None, None]]
            for j in range(2):
                at = slice(j * LANES, (j + 1) * LANES)
                here = slice(t, t + CHUNK)
                o_real, o_imag = patch[0, here, at], patch[1, here, at]
                for m in range(2):
                    of = slice((2 * h + m) * half + u, (2 * h + m) * half + u + CHUNK)
                    g = []
                    for c in range(2):
                        e = grad_even[of, c * half : (c + 1) * half]
                        o = grad_odd[of, c * half : (c + 1) * half]
                        g.append(e + o if j == 0 else e - o)
                    p_real, p_imag = probe[m, 0, here, at], probe[m, 1, here, at]
                    add_real = p_real * g[0] + p_imag * g[1]
                    add_imag = p_real * g[1] - p_imag * g[0]
                    terms[0][j] = add_real if m == 0 else terms[0][j] + add_real
                    terms[1][j] = add_imag if m == 0 else terms[1][j] + add_imag
                    probe_out[m, 0, here, at] += o_real * g[0] + o_imag * g[1]
                    probe_out[m, 1, here, at] += o_real * g[1] - o_imag * g[0]
            for c in range(2):
                first = pltpu.roll(terms[c][0], lane_at, 1)
                second = pltpu.roll(terms[c][1], lane_at, 1)
                spread = (
                    jnp.where(after, first, 0.0),
                    jnp.where(after, second, first),
                    jnp.where(after, 0.0, second),
                )
                for j in range(3):
                    acc[c, panel + j, pl.ds(row_at + t, CHUNK), :] += spread[j]
        return carry

    lax.fori_loop(0, counts[0], visit, 0)

    for c in range(2):
        for j in range(own):
            at = slice(j * LANES, (j + 1) * LANES)
            main_out[c, :, at] = acc[c, j, :rows, :]
            below_out[c, :, at] = acc[c, j, rows:, :].astype(bf16)
        for j in range(own, wide):
            at = slice((j - own) * LANES, (j - own + 1) * LANES)
            right_out[c, :, at] = acc[c, j, :rows, :].astype(bf16)
            corner_out[c, :, at] = acc[c, j, rows:, :].astype(bf16)


def exchange_kernel(
    sample, main, right_grad, below_grad, corner_grad, probe, probe_grad,
    sample_out, probe_out,
    from_left, from_above, from_both, parts, col_buf, row_buf, col_sum, row_sum, gathered, whole,
    halo_send, halo_recv, col_send, col_recv, row_send, row_recv,
    row_send2, row_recv2, col_send2, col_recv2,
    *, n_row, n_col, rate,
):
    f32, bf16 = jnp.float32, jnp.bfloat16
    frame = probe.shape[-1]
    row, col = lax.axis_index("row"), lax.axis_index("col")
    col_chunk = parts.shape[0] // n_col
    row_chunk = col_chunk // n_row

    def on_row(k):
        return (lax.rem(row + k, n_row), col)

    def on_col(k):
        return (row, lax.rem(col + k, n_col))

    def copy(src, dst, send, recv, to):
        return pltpu.make_async_remote_copy(
            src_ref=src, dst_ref=dst, send_sem=send, recv_sem=recv,
            device_id=to, device_id_type=pl.DeviceIdType.MESH,
        )

    barrier = pltpu.get_barrier_semaphore()
    down_right = (lax.rem(row + 1, n_row), lax.rem(col + 1, n_col))
    up_left = (lax.rem(row + n_row - 1, n_row), lax.rem(col + n_col - 1, n_col))
    peers = [on_row(k) for k in range(1, n_row)] + [on_col(k) for k in range(1, n_col)]
    peers += [down_right, up_left]
    for peer in peers:
        pl.semaphore_signal(barrier, inc=1, device_id=peer, device_id_type=pl.DeviceIdType.MESH)

    panels = frame // LANES
    blocks = [(m, c, j) for m in range(2) for c in range(2) for j in range(panels)]
    for b, (m, c, j) in enumerate(blocks):
        value = probe_grad[m, c, :, j * LANES : (j + 1) * LANES]
        parts[b * frame : (b + 1) * frame, :] = value.astype(bf16)
    pl.semaphore_wait(barrier, len(peers))

    def rows_of(index, size):
        return pl.ds(pl.multiple_of(index * size, 16), size)

    scatter = [
        copy(
            parts.at[rows_of(lax.rem(col + k, n_col), col_chunk)], col_buf.at[k],
            col_send.at[k], col_recv.at[k], on_col(k),
        )
        for k in range(1, n_col)
    ]
    for one in scatter:
        one.start()

    gives_right, gives_below = col < n_col - 1, row < n_row - 1
    has_left, has_above = col > 0, row > 0
    halos = [
        (copy(right_grad, from_left, halo_send.at[0], halo_recv.at[0], on_col(1)),
         gives_right, has_left),
        (copy(below_grad, from_above, halo_send.at[1], halo_recv.at[1], on_row(1)),
         gives_below, has_above),
        (copy(corner_grad, from_both, halo_send.at[2], halo_recv.at[2], down_right),
         jnp.logical_and(gives_right, gives_below), jnp.logical_and(has_left, has_above)),
    ]
    for one, gives, _ in halos:
        pl.when(gives)(one.start)

    for one in scatter:
        one.wait_recv()
    total = parts[rows_of(col, col_chunk), :].astype(f32)
    for k in range(1, n_col):
        total = total + col_buf[k].astype(f32)
    col_sum[...] = total.astype(bf16)
    reduce_rows = [
        copy(
            col_sum.at[rows_of(lax.rem(row + k, n_row), row_chunk)], row_buf.at[k],
            row_send.at[k], row_recv.at[k], on_row(k),
        )
        for k in range(1, n_row)
    ]
    for one in reduce_rows:
        one.start()

    power = probe[0, 0] ** 2 + probe[0, 1] ** 2 + (probe[1, 0] ** 2 + probe[1, 1] ** 2)
    scale = 1.0 / (jnp.max(power, keepdims=True) + 1e-06)
    for c in range(2):
        sample_out[c] = sample[c] - main[c] * scale

    for one in reduce_rows:
        one.wait_recv()
    total = col_sum[rows_of(row, row_chunk), :].astype(f32)
    for k in range(1, n_row):
        total = total + row_buf[k].astype(f32)
    row_sum[...] = total.astype(bf16)
    gather_rows = [
        copy(
            row_sum, gathered.at[rows_of(row, row_chunk)],
            row_send2.at[k], row_recv2.at[k], on_row(k),
        )
        for k in range(1, n_row)
    ]
    for one in gather_rows:
        one.start()
    gathered[rows_of(row, row_chunk), :] = row_sum[...]
    for one in gather_rows:
        one.wait_recv()
    gather_cols = [
        copy(
            gathered, whole.at[rows_of(col, col_chunk)],
            col_send2.at[k], col_recv2.at[k], on_col(k),
        )
        for k in range(1, n_col)
    ]
    for one in gather_cols:
        one.start()
    whole[rows_of(col, col_chunk), :] = gathered[...]

    def take(one, has, src, rows, cols):
        @pl.when(has)
        def _():
            one.wait_recv()
            for c in range(2):
                sample_out[c, :rows, :cols] -= src[c].astype(f32) * scale

    take(halos[0][0], halos[0][2], from_left, *from_left.shape[1:])
    take(halos[1][0], halos[1][2], from_above, *from_above.shape[1:])
    take(halos[2][0], halos[2][2], from_both, *from_both.shape[1:])

    for one in gather_cols:
        one.wait_recv()
    for b, (m, c, j) in enumerate(blocks):
        at = slice(j * LANES, (j + 1) * LANES)
        summed = whole[b * frame : (b + 1) * frame, :].astype(f32)
        probe_out[m, c, :, at] = probe[m, c, :, at] - rate * summed
    for one in scatter + reduce_rows + gather_rows + gather_cols:
        one.wait_send()
    for one, gives, _ in halos:
        pl.when(gives)(one.wait_send)


def shards(sample, probe_modes, amplitude, offsets, counts):
    frame = probe_modes.shape[-1]
    rows, cols = sample.shape[1:]
    slots = amplitude.shape[2]
    f32, bf16 = jnp.float32, jnp.bfloat16
    edge = sample.astype(bf16)
    right = shifted(edge[:, :, :frame], ("row", "col"), (0, -1))
    below = shifted(edge[:, :frame, :], ("row", "col"), (-1, 0))
    corner = shifted(edge[:, :frame, :frame], ("row", "col"), (-1, -1))
    panels = (cols + frame) // LANES
    shape = jax.ShapeDtypeStruct
    vmem = pl.BlockSpec(memory_space=pltpu.VMEM)
    smem = pl.BlockSpec(memory_space=pltpu.SMEM)
    main, right_grad, below_grad, corner_grad, probe_grad = pl.pallas_call(
        gradient_kernel,
        out_shape=(
            shape((2, rows, cols), f32),
            shape((2, rows, frame), bf16),
            shape((2, frame, cols), bf16),
            shape((2, frame, frame), bf16),
            shape(probe_modes.shape, f32),
        ),
        in_specs=[smem, smem] + [vmem] * 7,
        out_specs=(vmem,) * 5,
        scratch_shapes=[
            pltpu.VMEM((2, panels, rows + frame, LANES), f32),
            pltpu.VMEM((2, panels, rows + frame, LANES), f32),
            pltpu.VMEM((2, frame, frame), f32),
            pltpu.VMEM((2, frame, 2 * frame), bf16),
            pltpu.VMEM((2, 2 * frame, frame), bf16),
            pltpu.VMEM((2, frame, 2 * frame), bf16),
            pltpu.VMEM((2, 2 * frame, frame), bf16),
        ],
        compiler_params=pltpu.CompilerParams(vmem_limit_bytes=48 * 1024 * 1024),
    )(
        offsets.reshape(-1), counts.reshape(-1), jnp.asarray(tables(frame)), sample,
        right, below, corner, probe_modes, amplitude.reshape(slots, frame, frame),
    )
    n_row, n_col = lax.axis_size("row"), lax.axis_size("col")
    lines = probe_modes.size // LANES
    col_chunk = lines // n_col
    row_chunk = col_chunk // n_row
    dma = pltpu.SemaphoreType.DMA
    return pl.pallas_call(
        functools.partial(
            exchange_kernel, n_row=n_row, n_col=n_col, rate=1.0 / math.sqrt(n_row * n_col * slots)
        ),
        out_shape=(shape(sample.shape, f32), shape(probe_modes.shape, f32)),
        in_specs=[vmem] * 7,
        out_specs=(vmem,) * 2,
        scratch_shapes=[
            pltpu.VMEM((2, rows, frame), bf16),
            pltpu.VMEM((2, frame, cols), bf16),
            pltpu.VMEM((2, frame, frame), bf16),
            pltpu.VMEM((lines, LANES), bf16),
            pltpu.VMEM((n_col, col_chunk, LANES), bf16),
            pltpu.VMEM((n_row, row_chunk, LANES), bf16),
            pltpu.VMEM((col_chunk, LANES), bf16),
            pltpu.VMEM((row_chunk, LANES), bf16),
            pltpu.VMEM((col_chunk, LANES), bf16),
            pltpu.VMEM((lines, LANES), bf16),
            dma((3,)), dma((3,)),
            dma((n_col,)), dma((n_col,)), dma((n_row,)), dma((n_row,)),
            dma((n_row,)), dma((n_row,)), dma((n_col,)), dma((n_col,)),
        ],
        compiler_params=pltpu.CompilerParams(
            collective_id=0, has_side_effects=True, vmem_limit_bytes=48 * 1024 * 1024
        ),
    )(sample, main, right_grad, below_grad, corner_grad, probe_modes, probe_grad)


def solution(mesh):
    in_specs = (
        P(None, "row", "col"),
        P(),
        P("row", "col", None, None, None),
        P("row", "col", None, None),
        P("row", "col"),
    )
    out_specs = (P(None, "row", "col"), P())
    return jax.shard_map(shards, mesh=mesh, in_specs=in_specs, out_specs=out_specs, check_vma=False)
```

```python
import functools
import math

import jax
import jax.numpy as jnp
import ml_dtypes
import numpy as np
from jax import lax
from jax.experimental import pallas as pl
from jax.experimental.pallas import tpu as pltpu
from jax.sharding import PartitionSpec as P

LANES = 128
CHUNK = 16


def tables(frame):
    index = np.arange(frame)
    angle = 2.0 * math.pi / frame * ((index[:, None] * index[None, :]) % frame)
    scale = 1.0 / math.sqrt(frame)
    w_real, w_imag = np.cos(angle) * scale, -np.sin(angle) * scale

    def block(first):
        real, imag = w_real[first::2, : frame // 2], w_imag[first::2, : frame // 2]
        return np.block([[real, -imag], [imag, real]])

    even, odd = block(0), block(1)
    order = np.concatenate([index[0::2], index[1::2]])
    pick = np.eye(frame)[order]
    stack = np.stack([even, odd, even.T, odd.T, pick, pick.T])
    return stack.astype(np.float32).astype(ml_dtypes.bfloat16)


def halo_kernel(
    sample, right_out, below_out, corner_out,
    right_in, below_in, corner_in, edge, edge_below, edge_corner, send, recv,
    *, n_row, n_col,
):
    bf16 = jnp.bfloat16
    frame = right_out.shape[-1]
    row, col = lax.axis_index("row"), lax.axis_index("col")
    left = (row, lax.rem(col + n_col - 1, n_col))
    right = (row, lax.rem(col + 1, n_col))
    up = (lax.rem(row + n_row - 1, n_row), col)
    down = (lax.rem(row + 1, n_row), col)
    up_left = (up[0], left[1])
    down_right = (down[0], right[1])
    barrier = pltpu.get_barrier_semaphore()
    peers = (left, right, up, down, up_left, down_right)
    for peer in peers:
        pl.semaphore_signal(barrier, inc=1, device_id=peer, device_id_type=pl.DeviceIdType.MESH)
    edge[...] = sample[:, :, :frame].astype(bf16)
    edge_below[...] = sample[:, :frame, :].astype(bf16)
    edge_corner[...] = sample[:, :frame, :frame].astype(bf16)
    pl.semaphore_wait(barrier, len(peers))
    to_left, to_up = col > 0, row > 0
    has_right, has_below = col < n_col - 1, row < n_row - 1
    plan = [
        (edge, right_in, left, to_left, has_right, right_out),
        (edge_below, below_in, up, to_up, has_below, below_out),
        (edge_corner, corner_in, up_left, jnp.logical_and(to_left, to_up),
         jnp.logical_and(has_right, has_below), corner_out),
    ]
    copies = [
        pltpu.make_async_remote_copy(
            src_ref=src, dst_ref=dst, send_sem=send.at[i], recv_sem=recv.at[i],
            device_id=to, device_id_type=pl.DeviceIdType.MESH,
        )
        for i, (src, dst, to, _, _, _) in enumerate(plan)
    ]
    for one, item in zip(copies, plan):
        pl.when(item[3])(one.start)

    def finish(one, dst, has, out):
        @pl.when(has)
        def _():
            one.wait_recv()
            out[...] = dst[...]

        @pl.when(jnp.logical_not(has))
        def _():
            out[...] = jnp.zeros_like(out)

    for one, item in zip(copies, plan):
        finish(one, item[1], item[4], item[5])
    for one, item in zip(copies, plan):
        pl.when(item[3])(one.wait_send)


def gradient_kernel(
    offsets, counts, table, sample, right, below, corner, probe, amplitude,
    main_out, right_out, below_out, corner_out, probe_out,
    ext, acc, patch, xs, ys, zs, gs,
):
    rows, cols = sample.shape[1:]
    frame = probe.shape[-1]
    half = frame // 2
    own = cols // LANES
    wide = ext.shape[1]
    f32, bf16 = jnp.float32, jnp.bfloat16

    for c in range(2):
        for j in range(own):
            at = slice(j * LANES, (j + 1) * LANES)
            ext[c, j, :rows, :] = sample[c, :, at]
            ext[c, j, rows:, :] = below[c, :, at].astype(f32)
        for j in range(own, wide):
            at = slice((j - own) * LANES, (j - own + 1) * LANES)
            ext[c, j, :rows, :] = right[c, :, at].astype(f32)
            ext[c, j, rows:, :] = corner[c, :, at].astype(f32)
    acc[...] = jnp.zeros_like(acc)
    probe_out[...] = jnp.zeros_like(probe_out)

    def dot(a, b):
        return jnp.dot(a, b, preferred_element_type=f32)

    def visit(slot, carry):
        row_at = offsets[2 * slot]
        col_at = offsets[2 * slot + 1]
        panel = col_at // LANES
        lane_at = col_at % LANES
        back_by = lax.rem(LANES - lane_at, LANES)
        lane = lax.broadcasted_iota(jnp.int32, (CHUNK, LANES), 1)
        inside = lane < LANES - lane_at
        after = lane >= lane_at

        measured = dot(table[4], amplitude[slot]).astype(bf16)
        measured = dot(measured, table[5])

        def window(c, t):
            parts = [
                pltpu.roll(ext[c, panel + j, pl.ds(row_at + t, CHUNK), :], back_by, 1)
                for j in range(3)
            ]
            return [jnp.where(inside, parts[j], parts[j + 1]) for j in range(2)]

        for t in range(0, half, CHUNK):
            waves = []
            for h in range(2):
                u = h * half + t
                o_real, o_imag = window(0, u), window(1, u)
                wave = {}
                for j in range(2):
                    at = slice(j * LANES, (j + 1) * LANES)
                    patch[0, u : u + CHUNK, at] = o_real[j]
                    patch[1, u : u + CHUNK, at] = o_imag[j]
                    for m in range(2):
                        p_real = probe[m, 0, u : u + CHUNK, at]
                        p_imag = probe[m, 1, u : u + CHUNK, at]
                        wave[m, j, 0] = p_real * o_real[j] - p_imag * o_imag[j]
                        wave[m, j, 1] = p_real * o_imag[j] + p_imag * o_real[j]
                waves.append(wave)
            for m in range(2):
                for j in range(2):
                    at = slice(m * frame + j * LANES, m * frame + (j + 1) * LANES)
                    for c in range(2):
                        low, high = waves[0][m, j, c], waves[1][m, j, c]
                        to = slice(c * half + t, c * half + t + CHUNK)
                        xs[0, to, at] = (low + high).astype(bf16)
                        xs[1, to, at] = (low - high).astype(bf16)

        for p in range(2):
            product = dot(table[p], xs[p])
            for m in range(2):
                to = slice((2 * p + m) * half, (2 * p + m + 1) * half)
                for c in range(2):
                    value = product[c * half : (c + 1) * half, m * frame : (m + 1) * frame]
                    low, high = value[:, :half], value[:, half:]
                    at = slice(c * half, (c + 1) * half)
                    ys[0, to, at] = (low + high).astype(bf16)
                    ys[1, to, at] = (low - high).astype(bf16)

        for q in range(2):
            far = dot(ys[q], table[2 + q])
            for p in range(2):
                rows_of = [slice((2 * p + m) * half, (2 * p + m + 1) * half) for m in range(2)]
                fields = [[far[r, :half], far[r, half:]] for r in rows_of]
                intensity = sum(f[0] * f[0] + f[1] * f[1] for f in fields)
                level = measured[p * half : (p + 1) * half, q * half : (q + 1) * half]
                factor = 1.0 - level * lax.rsqrt(jnp.maximum(intensity, 0.0625))
                for m in range(2):
                    at = slice(m * frame + q * half, m * frame + (q + 1) * half)
                    for c in range(2):
                        zs[p, c * half : (c + 1) * half, at] = (fields[m][c] * factor).astype(bf16)

        from_even = dot(table[2], zs[0])
        from_odd = dot(table[3], zs[1])
        for h, back in enumerate((from_even + from_odd, from_even - from_odd)):
            for m in range(2):
                to = slice((2 * h + m) * half, (2 * h + m + 1) * half)
                for q in range(2):
                    at = slice(m * frame + q * half, m * frame + (q + 1) * half)
                    for c in range(2):
                        gs[q, to, c * half : (c + 1) * half] = back[
                            c * half : (c + 1) * half, at
                        ].astype(bf16)

        grad_even = dot(gs[0], table[0])
        grad_odd = dot(gs[1], table[1])
        for t in range(0, frame, CHUNK):
            h, u = divmod(t, half)
            terms = [[None, None], [None, None]]
            for j in range(2):
                at = slice(j * LANES, (j + 1) * LANES)
                here = slice(t, t + CHUNK)
                o_real, o_imag = patch[0, here, at], patch[1, here, at]
                for m in range(2):
                    of = slice((2 * h + m) * half + u, (2 * h + m) * half + u + CHUNK)
                    g = []
                    for c in range(2):
                        e = grad_even[of, c * half : (c + 1) * half]
                        o = grad_odd[of, c * half : (c + 1) * half]
                        g.append(e + o if j == 0 else e - o)
                    p_real, p_imag = probe[m, 0, here, at], probe[m, 1, here, at]
                    add_real = p_real * g[0] + p_imag * g[1]
                    add_imag = p_real * g[1] - p_imag * g[0]
                    terms[0][j] = add_real if m == 0 else terms[0][j] + add_real
                    terms[1][j] = add_imag if m == 0 else terms[1][j] + add_imag
                    probe_out[m, 0, here, at] += o_real * g[0] + o_imag * g[1]
                    probe_out[m, 1, here, at] += o_real * g[1] - o_imag * g[0]
            for c in range(2):
                first = pltpu.roll(terms[c][0], lane_at, 1)
                second = pltpu.roll(terms[c][1], lane_at, 1)
                spread = (
                    jnp.where(after, first, 0.0),
                    jnp.where(after, second, first),
                    jnp.where(after, 0.0, second),
                )
                for j in range(3):
                    acc[c, panel + j, pl.ds(row_at + t, CHUNK), :] += spread[j]
        return carry

    lax.fori_loop(0, counts[0], visit, 0)

    for c in range(2):
        for j in range(own):
            at = slice(j * LANES, (j + 1) * LANES)
            main_out[c, :, at] = acc[c, j, :rows, :]
            below_out[c, :, at] = acc[c, j, rows:, :].astype(bf16)
        for j in range(own, wide):
            at = slice((j - own) * LANES, (j - own + 1) * LANES)
            right_out[c, :, at] = acc[c, j, :rows, :].astype(bf16)
            corner_out[c, :, at] = acc[c, j, rows:, :].astype(bf16)


def exchange_kernel(
    sample, main, right_grad, below_grad, corner_grad, probe, probe_grad,
    sample_out, probe_out,
    from_left, from_above, from_both, parts, col_buf, row_buf, col_sum, row_sum, gathered, whole,
    halo_send, halo_recv, col_send, col_recv, row_send, row_recv,
    row_send2, row_recv2, col_send2, col_recv2,
    *, n_row, n_col, rate,
):
    f32, bf16 = jnp.float32, jnp.bfloat16
    frame = probe.shape[-1]
    row, col = lax.axis_index("row"), lax.axis_index("col")
    col_chunk = parts.shape[0] // n_col
    row_chunk = col_chunk // n_row

    def on_row(k):
        return (lax.rem(row + k, n_row), col)

    def on_col(k):
        return (row, lax.rem(col + k, n_col))

    def copy(src, dst, send, recv, to):
        return pltpu.make_async_remote_copy(
            src_ref=src, dst_ref=dst, send_sem=send, recv_sem=recv,
            device_id=to, device_id_type=pl.DeviceIdType.MESH,
        )

    barrier = pltpu.get_barrier_semaphore()
    down_right = (lax.rem(row + 1, n_row), lax.rem(col + 1, n_col))
    up_left = (lax.rem(row + n_row - 1, n_row), lax.rem(col + n_col - 1, n_col))
    peers = [on_row(k) for k in range(1, n_row)] + [on_col(k) for k in range(1, n_col)]
    peers += [down_right, up_left]
    for peer in peers:
        pl.semaphore_signal(barrier, inc=1, device_id=peer, device_id_type=pl.DeviceIdType.MESH)

    panels = frame // LANES
    blocks = [(m, c, j) for m in range(2) for c in range(2) for j in range(panels)]
    for b, (m, c, j) in enumerate(blocks):
        value = probe_grad[m, c, :, j * LANES : (j + 1) * LANES]
        parts[b * frame : (b + 1) * frame, :] = value.astype(bf16)
    pl.semaphore_wait(barrier, len(peers))

    def rows_of(index, size):
        return pl.ds(pl.multiple_of(index * size, 16), size)

    scatter = [
        copy(
            parts.at[rows_of(lax.rem(col + k, n_col), col_chunk)], col_buf.at[k],
            col_send.at[k], col_recv.at[k], on_col(k),
        )
        for k in range(1, n_col)
    ]
    for one in scatter:
        one.start()

    gives_right, gives_below = col < n_col - 1, row < n_row - 1
    has_left, has_above = col > 0, row > 0
    halos = [
        (copy(right_grad, from_left, halo_send.at[0], halo_recv.at[0], on_col(1)),
         gives_right, has_left),
        (copy(below_grad, from_above, halo_send.at[1], halo_recv.at[1], on_row(1)),
         gives_below, has_above),
        (copy(corner_grad, from_both, halo_send.at[2], halo_recv.at[2], down_right),
         jnp.logical_and(gives_right, gives_below), jnp.logical_and(has_left, has_above)),
    ]
    for one, gives, _ in halos:
        pl.when(gives)(one.start)

    for one in scatter:
        one.wait_recv()
    total = parts[rows_of(col, col_chunk), :].astype(f32)
    for k in range(1, n_col):
        total = total + col_buf[k].astype(f32)
    col_sum[...] = total
    reduce_rows = [
        copy(
            col_sum.at[rows_of(lax.rem(row + k, n_row), row_chunk)], row_buf.at[k],
            row_send.at[k], row_recv.at[k], on_row(k),
        )
        for k in range(1, n_row)
    ]
    for one in reduce_rows:
        one.start()

    power = probe[0, 0] ** 2 + probe[0, 1] ** 2 + (probe[1, 0] ** 2 + probe[1, 1] ** 2)
    scale = 1.0 / (jnp.max(power, keepdims=True) + 1e-06)
    for c in range(2):
        sample_out[c] = sample[c] - main[c] * scale

    for one in reduce_rows:
        one.wait_recv()
    total = col_sum[rows_of(row, row_chunk), :]
    for k in range(1, n_row):
        total = total + row_buf[k]
    row_sum[...] = total.astype(bf16)
    gather_rows = [
        copy(
            row_sum, gathered.at[rows_of(row, row_chunk)],
            row_send2.at[k], row_recv2.at[k], on_row(k),
        )
        for k in range(1, n_row)
    ]
    for one in gather_rows:
        one.start()
    gathered[rows_of(row, row_chunk), :] = row_sum[...]
    for one in gather_rows:
        one.wait_recv()
    gather_cols = [
        copy(
            gathered, whole.at[rows_of(col, col_chunk)],
            col_send2.at[k], col_recv2.at[k], on_col(k),
        )
        for k in range(1, n_col)
    ]
    for one in gather_cols:
        one.start()
    whole[rows_of(col, col_chunk), :] = gathered[...]

    def take(one, has, src, rows, cols):
        @pl.when(has)
        def _():
            one.wait_recv()
            for c in range(2):
                sample_out[c, :rows, :cols] -= src[c].astype(f32) * scale

    take(halos[0][0], halos[0][2], from_left, *from_left.shape[1:])
    take(halos[1][0], halos[1][2], from_above, *from_above.shape[1:])
    take(halos[2][0], halos[2][2], from_both, *from_both.shape[1:])

    for one in gather_cols:
        one.wait_recv()
    for b, (m, c, j) in enumerate(blocks):
        at = slice(j * LANES, (j + 1) * LANES)
        summed = whole[b * frame : (b + 1) * frame, :].astype(f32)
        probe_out[m, c, :, at] = probe[m, c, :, at] - rate * summed
    for one in scatter + reduce_rows + gather_rows + gather_cols:
        one.wait_send()
    for one, gives, _ in halos:
        pl.when(gives)(one.wait_send)


def shards(sample, probe_modes, amplitude, offsets, counts):
    frame = probe_modes.shape[-1]
    rows, cols = sample.shape[1:]
    slots = amplitude.shape[2]
    f32, bf16 = jnp.float32, jnp.bfloat16
    panels = (cols + frame) // LANES
    shape = jax.ShapeDtypeStruct
    vmem = pl.BlockSpec(memory_space=pltpu.VMEM)
    smem = pl.BlockSpec(memory_space=pltpu.SMEM)
    n_row, n_col = lax.axis_size("row"), lax.axis_size("col")
    dma = pltpu.SemaphoreType.DMA
    halo_shapes = ((2, rows, frame), (2, frame, cols), (2, frame, frame))
    right, below, corner = pl.pallas_call(
        functools.partial(halo_kernel, n_row=n_row, n_col=n_col),
        out_shape=tuple(shape(h, bf16) for h in halo_shapes),
        in_specs=[vmem],
        out_specs=(vmem,) * 3,
        scratch_shapes=[pltpu.VMEM(h, bf16) for h in halo_shapes * 2] + [dma((3,)), dma((3,))],
        compiler_params=pltpu.CompilerParams(
            collective_id=1, has_side_effects=True, vmem_limit_bytes=32 * 1024 * 1024
        ),
    )(sample)
    main, right_grad, below_grad, corner_grad, probe_grad = pl.pallas_call(
        gradient_kernel,
        out_shape=(
            shape((2, rows, cols), f32),
            shape((2, rows, frame), bf16),
            shape((2, frame, cols), bf16),
            shape((2, frame, frame), bf16),
            shape(probe_modes.shape, f32),
        ),
        in_specs=[smem, smem] + [vmem] * 7,
        out_specs=(vmem,) * 5,
        scratch_shapes=[
            pltpu.VMEM((2, panels, rows + frame, LANES), f32),
            pltpu.VMEM((2, panels, rows + frame, LANES), f32),
            pltpu.VMEM((2, frame, frame), f32),
            pltpu.VMEM((2, frame, 2 * frame), bf16),
            pltpu.VMEM((2, 2 * frame, frame), bf16),
            pltpu.VMEM((2, frame, 2 * frame), bf16),
            pltpu.VMEM((2, 2 * frame, frame), bf16),
        ],
        compiler_params=pltpu.CompilerParams(vmem_limit_bytes=48 * 1024 * 1024),
    )(
        offsets.reshape(-1), counts.reshape(-1), jnp.asarray(tables(frame)), sample,
        right, below, corner, probe_modes, amplitude.reshape(slots, frame, frame),
    )
    lines = probe_modes.size // LANES
    col_chunk = lines // n_col
    row_chunk = col_chunk // n_row
    return pl.pallas_call(
        functools.partial(
            exchange_kernel, n_row=n_row, n_col=n_col, rate=1.0 / math.sqrt(n_row * n_col * slots)
        ),
        out_shape=(shape(sample.shape, f32), shape(probe_modes.shape, f32)),
        in_specs=[vmem] * 7,
        out_specs=(vmem,) * 2,
        scratch_shapes=[
            pltpu.VMEM((2, rows, frame), bf16),
            pltpu.VMEM((2, frame, cols), bf16),
            pltpu.VMEM((2, frame, frame), bf16),
            pltpu.VMEM((lines, LANES), bf16),
            pltpu.VMEM((n_col, col_chunk, LANES), bf16),
            pltpu.VMEM((n_row, row_chunk, LANES), f32),
            pltpu.VMEM((col_chunk, LANES), f32),
            pltpu.VMEM((row_chunk, LANES), bf16),
            pltpu.VMEM((col_chunk, LANES), bf16),
            pltpu.VMEM((lines, LANES), bf16),
            dma((3,)), dma((3,)),
            dma((n_col,)), dma((n_col,)), dma((n_row,)), dma((n_row,)),
            dma((n_row,)), dma((n_row,)), dma((n_col,)), dma((n_col,)),
        ],
        compiler_params=pltpu.CompilerParams(
            collective_id=0, has_side_effects=True, vmem_limit_bytes=48 * 1024 * 1024
        ),
    )(sample, main, right_grad, below_grad, corner_grad, probe_modes, probe_grad)


def solution(mesh):
    in_specs = (
        P(None, "row", "col"),
        P(),
        P("row", "col", None, None, None),
        P("row", "col", None, None),
        P("row", "col"),
    )
    out_specs = (P(None, "row", "col"), P())
    return jax.shard_map(shards, mesh=mesh, in_specs=in_specs, out_specs=out_specs, check_vma=False)
```

```python
import functools
import math

import jax
import jax.numpy as jnp
import ml_dtypes
import numpy as np
from jax import lax
from jax.experimental import pallas as pl
from jax.experimental.pallas import tpu as pltpu
from jax.sharding import PartitionSpec as P

LANES = 128
CHUNK = 16


def tables(frame):
    index = np.arange(frame)
    angle = 2.0 * math.pi / frame * ((index[:, None] * index[None, :]) % frame)
    scale = 1.0 / math.sqrt(frame)
    w_real, w_imag = np.cos(angle) * scale, -np.sin(angle) * scale

    def block(first):
        real, imag = w_real[first::2, : frame // 2], w_imag[first::2, : frame // 2]
        return np.block([[real, -imag], [imag, real]])

    even, odd = block(0), block(1)
    order = np.concatenate([index[0::2], index[1::2]])
    pick = np.eye(frame)[order]
    stack = np.stack([even, odd, even.T, odd.T, pick, pick.T])
    return stack.astype(np.float32).astype(ml_dtypes.bfloat16)


def halo_kernel(
    sample, right_out, below_out, corner_out,
    right_in, below_in, corner_in, edge, edge_below, edge_corner, send, recv,
    *, n_row, n_col,
):
    bf16 = jnp.bfloat16
    frame = right_out.shape[-1]
    row, col = lax.axis_index("row"), lax.axis_index("col")
    left = (row, lax.rem(col + n_col - 1, n_col))
    right = (row, lax.rem(col + 1, n_col))
    up = (lax.rem(row + n_row - 1, n_row), col)
    down = (lax.rem(row + 1, n_row), col)
    up_left = (up[0], left[1])
    down_right = (down[0], right[1])
    barrier = pltpu.get_barrier_semaphore()
    peers = (left, right, up, down, up_left, down_right)
    for peer in peers:
        pl.semaphore_signal(barrier, inc=1, device_id=peer, device_id_type=pl.DeviceIdType.MESH)
    edge[...] = sample[:, :, :frame].astype(bf16)
    edge_below[...] = sample[:, :frame, :].astype(bf16)
    edge_corner[...] = sample[:, :frame, :frame].astype(bf16)
    pl.semaphore_wait(barrier, len(peers))
    to_left, to_up = col > 0, row > 0
    has_right, has_below = col < n_col - 1, row < n_row - 1
    plan = [
        (edge, right_in, left, to_left, has_right, right_out),
        (edge_below, below_in, up, to_up, has_below, below_out),
        (edge_corner, corner_in, up_left, jnp.logical_and(to_left, to_up),
         jnp.logical_and(has_right, has_below), corner_out),
    ]
    copies = [
        pltpu.make_async_remote_copy(
            src_ref=src, dst_ref=dst, send_sem=send.at[i], recv_sem=recv.at[i],
            device_id=to, device_id_type=pl.DeviceIdType.MESH,
        )
        for i, (src, dst, to, _, _, _) in enumerate(plan)
    ]
    for one, item in zip(copies, plan):
        pl.when(item[3])(one.start)

    def finish(one, dst, has, out):
        @pl.when(has)
        def _():
            one.wait_recv()
            out[...] = dst[...]

        @pl.when(jnp.logical_not(has))
        def _():
            out[...] = jnp.zeros_like(out)

    for one, item in zip(copies, plan):
        finish(one, item[1], item[4], item[5])
    for one, item in zip(copies, plan):
        pl.when(item[3])(one.wait_send)


def gradient_kernel(
    offsets, counts, table, sample, right, below, corner, probe, amplitude,
    main_out, right_out, below_out, corner_out, probe_out,
    ext, acc, *pairs,
):
    rows, cols = sample.shape[1:]
    frame = probe.shape[-1]
    half = frame // 2
    own = cols // LANES
    wide = ext.shape[1]
    f32, bf16 = jnp.float32, jnp.bfloat16

    for c in range(2):
        for j in range(own):
            at = slice(j * LANES, (j + 1) * LANES)
            ext[c, j, :rows, :] = sample[c, :, at]
            ext[c, j, rows:, :] = below[c, :, at].astype(f32)
        for j in range(own, wide):
            at = slice((j - own) * LANES, (j - own + 1) * LANES)
            ext[c, j, :rows, :] = right[c, :, at].astype(f32)
            ext[c, j, rows:, :] = corner[c, :, at].astype(f32)
    acc[...] = jnp.zeros_like(acc)
    probe_out[...] = jnp.zeros_like(probe_out)

    def dot(a, b):
        return jnp.dot(a, b, preferred_element_type=f32)

    def visit(slot, turn):
        patch, xs, ys, zs, gs = (ref.at[turn] for ref in pairs)
        row_at = offsets[2 * slot]
        col_at = offsets[2 * slot + 1]
        panel = col_at // LANES
        lane_at = col_at % LANES
        back_by = lax.rem(LANES - lane_at, LANES)
        lane = lax.broadcasted_iota(jnp.int32, (CHUNK, LANES), 1)
        inside = lane < LANES - lane_at
        after = lane >= lane_at

        measured = dot(table[4], amplitude[slot]).astype(bf16)
        measured = dot(measured, table[5])

        def window(c, t):
            parts = [
                pltpu.roll(ext[c, panel + j, pl.ds(row_at + t, CHUNK), :], back_by, 1)
                for j in range(3)
            ]
            return [jnp.where(inside, parts[j], parts[j + 1]) for j in range(2)]

        for t in range(0, half, CHUNK):
            waves = []
            for h in range(2):
                u = h * half + t
                o_real, o_imag = window(0, u), window(1, u)
                wave = {}
                for j in range(2):
                    at = slice(j * LANES, (j + 1) * LANES)
                    patch[0, u : u + CHUNK, at] = o_real[j]
                    patch[1, u : u + CHUNK, at] = o_imag[j]
                    for m in range(2):
                        p_real = probe[m, 0, u : u + CHUNK, at]
                        p_imag = probe[m, 1, u : u + CHUNK, at]
                        wave[m, j, 0] = p_real * o_real[j] - p_imag * o_imag[j]
                        wave[m, j, 1] = p_real * o_imag[j] + p_imag * o_real[j]
                waves.append(wave)
            for m in range(2):
                for j in range(2):
                    at = slice(m * frame + j * LANES, m * frame + (j + 1) * LANES)
                    for c in range(2):
                        low, high = waves[0][m, j, c], waves[1][m, j, c]
                        to = slice(c * half + t, c * half + t + CHUNK)
                        xs[0, to, at] = (low + high).astype(bf16)
                        xs[1, to, at] = (low - high).astype(bf16)

        yield
        for p in range(2):
            product = dot(table[p], xs[p])
            for m in range(2):
                to = slice((2 * p + m) * half, (2 * p + m + 1) * half)
                for c in range(2):
                    value = product[c * half : (c + 1) * half, m * frame : (m + 1) * frame]
                    low, high = value[:, :half], value[:, half:]
                    at = slice(c * half, (c + 1) * half)
                    ys[0, to, at] = (low + high).astype(bf16)
                    ys[1, to, at] = (low - high).astype(bf16)

        yield
        for q in range(2):
            far = dot(ys[q], table[2 + q])
            for p in range(2):
                rows_of = [slice((2 * p + m) * half, (2 * p + m + 1) * half) for m in range(2)]
                fields = [[far[r, :half], far[r, half:]] for r in rows_of]
                intensity = sum(f[0] * f[0] + f[1] * f[1] for f in fields)
                level = measured[p * half : (p + 1) * half, q * half : (q + 1) * half]
                factor = 1.0 - level * lax.rsqrt(jnp.maximum(intensity, 0.0625))
                for m in range(2):
                    at = slice(m * frame + q * half, m * frame + (q + 1) * half)
                    for c in range(2):
                        zs[p, c * half : (c + 1) * half, at] = (fields[m][c] * factor).astype(bf16)

        yield
        from_even = dot(table[2], zs[0])
        from_odd = dot(table[3], zs[1])
        for h, back in enumerate((from_even + from_odd, from_even - from_odd)):
            for m in range(2):
                to = slice((2 * h + m) * half, (2 * h + m + 1) * half)
                for q in range(2):
                    at = slice(m * frame + q * half, m * frame + (q + 1) * half)
                    for c in range(2):
                        gs[q, to, c * half : (c + 1) * half] = back[
                            c * half : (c + 1) * half, at
                        ].astype(bf16)

        yield
        grad_even = dot(gs[0], table[0])
        grad_odd = dot(gs[1], table[1])
        for t in range(0, frame, CHUNK):
            h, u = divmod(t, half)
            terms = [[None, None], [None, None]]
            for j in range(2):
                at = slice(j * LANES, (j + 1) * LANES)
                here = slice(t, t + CHUNK)
                o_real, o_imag = patch[0, here, at], patch[1, here, at]
                for m in range(2):
                    of = slice((2 * h + m) * half + u, (2 * h + m) * half + u + CHUNK)
                    g = []
                    for c in range(2):
                        e = grad_even[of, c * half : (c + 1) * half]
                        o = grad_odd[of, c * half : (c + 1) * half]
                        g.append(e + o if j == 0 else e - o)
                    p_real, p_imag = probe[m, 0, here, at], probe[m, 1, here, at]
                    add_real = p_real * g[0] + p_imag * g[1]
                    add_imag = p_real * g[1] - p_imag * g[0]
                    terms[0][j] = add_real if m == 0 else terms[0][j] + add_real
                    terms[1][j] = add_imag if m == 0 else terms[1][j] + add_imag
                    probe_out[m, 0, here, at] += o_real * g[0] + o_imag * g[1]
                    probe_out[m, 1, here, at] += o_real * g[1] - o_imag * g[0]
            for c in range(2):
                first = pltpu.roll(terms[c][0], lane_at, 1)
                second = pltpu.roll(terms[c][1], lane_at, 1)
                spread = (
                    jnp.where(after, first, 0.0),
                    jnp.where(after, second, first),
                    jnp.where(after, 0.0, second),
                )
                for j in range(3):
                    acc[c, panel + j, pl.ds(row_at + t, CHUNK), :] += spread[j]
        yield

    def both(pair, carry):
        first, second = visit(2 * pair, 0), visit(2 * pair + 1, 1)
        next(first)
        for _ in range(4):
            next(first)
            next(second)
        next(second)
        return carry

    live = counts[0]
    lax.fori_loop(0, live // 2, both, 0)

    @pl.when(live % 2 == 1)
    def _():
        for _ in visit(live - 1, 0):
            pass

    for c in range(2):
        for j in range(own):
            at = slice(j * LANES, (j + 1) * LANES)
            main_out[c, :, at] = acc[c, j, :rows, :]
            below_out[c, :, at] = acc[c, j, rows:, :].astype(bf16)
        for j in range(own, wide):
            at = slice((j - own) * LANES, (j - own + 1) * LANES)
            right_out[c, :, at] = acc[c, j, :rows, :].astype(bf16)
            corner_out[c, :, at] = acc[c, j, rows:, :].astype(bf16)


def exchange_kernel(
    sample, main, right_grad, below_grad, corner_grad, probe, probe_grad,
    sample_out, probe_out,
    from_left, from_above, from_both, parts, col_buf, row_buf, col_sum, row_sum, gathered, whole,
    halo_send, halo_recv, col_send, col_recv, row_send, row_recv,
    row_send2, row_recv2, col_send2, col_recv2,
    *, n_row, n_col, rate,
):
    f32, bf16 = jnp.float32, jnp.bfloat16
    frame = probe.shape[-1]
    row, col = lax.axis_index("row"), lax.axis_index("col")
    col_chunk = parts.shape[0] // n_col
    row_chunk = col_chunk // n_row

    def on_row(k):
        return (lax.rem(row + k, n_row), col)

    def on_col(k):
        return (row, lax.rem(col + k, n_col))

    def copy(src, dst, send, recv, to):
        return pltpu.make_async_remote_copy(
            src_ref=src, dst_ref=dst, send_sem=send, recv_sem=recv,
            device_id=to, device_id_type=pl.DeviceIdType.MESH,
        )

    barrier = pltpu.get_barrier_semaphore()
    down_right = (lax.rem(row + 1, n_row), lax.rem(col + 1, n_col))
    up_left = (lax.rem(row + n_row - 1, n_row), lax.rem(col + n_col - 1, n_col))
    peers = [on_row(k) for k in range(1, n_row)] + [on_col(k) for k in range(1, n_col)]
    peers += [down_right, up_left]
    for peer in peers:
        pl.semaphore_signal(barrier, inc=1, device_id=peer, device_id_type=pl.DeviceIdType.MESH)

    panels = frame // LANES
    blocks = [(m, c, j) for m in range(2) for c in range(2) for j in range(panels)]
    for b, (m, c, j) in enumerate(blocks):
        value = probe_grad[m, c, :, j * LANES : (j + 1) * LANES]
        parts[b * frame : (b + 1) * frame, :] = value.astype(bf16)
    pl.semaphore_wait(barrier, len(peers))

    def rows_of(index, size):
        return pl.ds(pl.multiple_of(index * size, 16), size)

    scatter = [
        copy(
            parts.at[rows_of(lax.rem(col + k, n_col), col_chunk)], col_buf.at[k],
            col_send.at[k], col_recv.at[k], on_col(k),
        )
        for k in range(1, n_col)
    ]
    for one in scatter:
        one.start()

    gives_right, gives_below = col < n_col - 1, row < n_row - 1
    has_left, has_above = col > 0, row > 0
    halos = [
        (copy(right_grad, from_left, halo_send.at[0], halo_recv.at[0], on_col(1)),
         gives_right, has_left),
        (copy(below_grad, from_above, halo_send.at[1], halo_recv.at[1], on_row(1)),
         gives_below, has_above),
        (copy(corner_grad, from_both, halo_send.at[2], halo_recv.at[2], down_right),
         jnp.logical_and(gives_right, gives_below), jnp.logical_and(has_left, has_above)),
    ]
    for one, gives, _ in halos:
        pl.when(gives)(one.start)

    for one in scatter:
        one.wait_recv()
    total = parts[rows_of(col, col_chunk), :].astype(f32)
    for k in range(1, n_col):
        total = total + col_buf[k].astype(f32)
    col_sum[...] = total
    reduce_rows = [
        copy(
            col_sum.at[rows_of(lax.rem(row + k, n_row), row_chunk)], row_buf.at[k],
            row_send.at[k], row_recv.at[k], on_row(k),
        )
        for k in range(1, n_row)
    ]
    for one in reduce_rows:
        one.start()

    power = probe[0, 0] ** 2 + probe[0, 1] ** 2 + (probe[1, 0] ** 2 + probe[1, 1] ** 2)
    scale = 1.0 / (jnp.max(power, keepdims=True) + 1e-06)
    for c in range(2):
        sample_out[c] = sample[c] - main[c] * scale

    for one in reduce_rows:
        one.wait_recv()
    total = col_sum[rows_of(row, row_chunk), :]
    for k in range(1, n_row):
        total = total + row_buf[k]
    row_sum[...] = total.astype(bf16)
    gather_rows = [
        copy(
            row_sum, gathered.at[rows_of(row, row_chunk)],
            row_send2.at[k], row_recv2.at[k], on_row(k),
        )
        for k in range(1, n_row)
    ]
    for one in gather_rows:
        one.start()
    gathered[rows_of(row, row_chunk), :] = row_sum[...]
    for one in gather_rows:
        one.wait_recv()
    gather_cols = [
        copy(
            gathered, whole.at[rows_of(col, col_chunk)],
            col_send2.at[k], col_recv2.at[k], on_col(k),
        )
        for k in range(1, n_col)
    ]
    for one in gather_cols:
        one.start()
    whole[rows_of(col, col_chunk), :] = gathered[...]

    def take(one, has, src, rows, cols):
        @pl.when(has)
        def _():
            one.wait_recv()
            for c in range(2):
                sample_out[c, :rows, :cols] -= src[c].astype(f32) * scale

    take(halos[0][0], halos[0][2], from_left, *from_left.shape[1:])
    take(halos[1][0], halos[1][2], from_above, *from_above.shape[1:])
    take(halos[2][0], halos[2][2], from_both, *from_both.shape[1:])

    for one in gather_cols:
        one.wait_recv()
    for b, (m, c, j) in enumerate(blocks):
        at = slice(j * LANES, (j + 1) * LANES)
        summed = whole[b * frame : (b + 1) * frame, :].astype(f32)
        probe_out[m, c, :, at] = probe[m, c, :, at] - rate * summed
    for one in scatter + reduce_rows + gather_rows + gather_cols:
        one.wait_send()
    for one, gives, _ in halos:
        pl.when(gives)(one.wait_send)


def shards(sample, probe_modes, amplitude, offsets, counts):
    frame = probe_modes.shape[-1]
    rows, cols = sample.shape[1:]
    slots = amplitude.shape[2]
    f32, bf16 = jnp.float32, jnp.bfloat16
    panels = (cols + frame) // LANES
    shape = jax.ShapeDtypeStruct
    vmem = pl.BlockSpec(memory_space=pltpu.VMEM)
    smem = pl.BlockSpec(memory_space=pltpu.SMEM)
    n_row, n_col = lax.axis_size("row"), lax.axis_size("col")
    dma = pltpu.SemaphoreType.DMA
    halo_shapes = ((2, rows, frame), (2, frame, cols), (2, frame, frame))
    right, below, corner = pl.pallas_call(
        functools.partial(halo_kernel, n_row=n_row, n_col=n_col),
        out_shape=tuple(shape(h, bf16) for h in halo_shapes),
        in_specs=[vmem],
        out_specs=(vmem,) * 3,
        scratch_shapes=[pltpu.VMEM(h, bf16) for h in halo_shapes * 2] + [dma((3,)), dma((3,))],
        compiler_params=pltpu.CompilerParams(
            collective_id=1, has_side_effects=True, vmem_limit_bytes=32 * 1024 * 1024
        ),
    )(sample)
    main, right_grad, below_grad, corner_grad, probe_grad = pl.pallas_call(
        gradient_kernel,
        out_shape=(
            shape((2, rows, cols), f32),
            shape((2, rows, frame), bf16),
            shape((2, frame, cols), bf16),
            shape((2, frame, frame), bf16),
            shape(probe_modes.shape, f32),
        ),
        in_specs=[smem, smem] + [vmem] * 7,
        out_specs=(vmem,) * 5,
        scratch_shapes=[
            pltpu.VMEM((2, panels, rows + frame, LANES), f32),
            pltpu.VMEM((2, panels, rows + frame, LANES), f32),
            pltpu.VMEM((2, 2, frame, frame), f32),
            pltpu.VMEM((2, 2, frame, 2 * frame), bf16),
            pltpu.VMEM((2, 2, 2 * frame, frame), bf16),
            pltpu.VMEM((2, 2, frame, 2 * frame), bf16),
            pltpu.VMEM((2, 2, 2 * frame, frame), bf16),
        ],
        compiler_params=pltpu.CompilerParams(vmem_limit_bytes=48 * 1024 * 1024),
    )(
        offsets.reshape(-1), counts.reshape(-1), jnp.asarray(tables(frame)), sample,
        right, below, corner, probe_modes, amplitude.reshape(slots, frame, frame),
    )
    lines = probe_modes.size // LANES
    col_chunk = lines // n_col
    row_chunk = col_chunk // n_row
    return pl.pallas_call(
        functools.partial(
            exchange_kernel, n_row=n_row, n_col=n_col, rate=1.0 / math.sqrt(n_row * n_col * slots)
        ),
        out_shape=(shape(sample.shape, f32), shape(probe_modes.shape, f32)),
        in_specs=[vmem] * 7,
        out_specs=(vmem,) * 2,
        scratch_shapes=[
            pltpu.VMEM((2, rows, frame), bf16),
            pltpu.VMEM((2, frame, cols), bf16),
            pltpu.VMEM((2, frame, frame), bf16),
            pltpu.VMEM((lines, LANES), bf16),
            pltpu.VMEM((n_col, col_chunk, LANES), bf16),
            pltpu.VMEM((n_row, row_chunk, LANES), f32),
            pltpu.VMEM((col_chunk, LANES), f32),
            pltpu.VMEM((row_chunk, LANES), bf16),
            pltpu.VMEM((col_chunk, LANES), bf16),
            pltpu.VMEM((lines, LANES), bf16),
            dma((3,)), dma((3,)),
            dma((n_col,)), dma((n_col,)), dma((n_row,)), dma((n_row,)),
            dma((n_row,)), dma((n_row,)), dma((n_col,)), dma((n_col,)),
        ],
        compiler_params=pltpu.CompilerParams(
            collective_id=0, has_side_effects=True, vmem_limit_bytes=48 * 1024 * 1024
        ),
    )(sample, main, right_grad, below_grad, corner_grad, probe_modes, probe_grad)


def solution(mesh):
    in_specs = (
        P(None, "row", "col"),
        P(),
        P("row", "col", None, None, None),
        P("row", "col", None, None),
        P("row", "col"),
    )
    out_specs = (P(None, "row", "col"), P())
    return jax.shard_map(shards, mesh=mesh, in_specs=in_specs, out_specs=out_specs, check_vma=False)
```

```python
import functools
import math

import jax
import jax.numpy as jnp
import ml_dtypes
import numpy as np
from jax import lax
from jax.experimental import pallas as pl
from jax.experimental.pallas import tpu as pltpu
from jax.sharding import PartitionSpec as P

LANES = 128
CHUNK = 16


def tables(frame):
    index = np.arange(frame)
    angle = 2.0 * math.pi / frame * ((index[:, None] * index[None, :]) % frame)
    scale = 1.0 / math.sqrt(frame)
    w_real, w_imag = np.cos(angle) * scale, -np.sin(angle) * scale

    def block(first):
        real, imag = w_real[first::2, : frame // 2], w_imag[first::2, : frame // 2]
        return np.block([[real, -imag], [imag, real]])

    even, odd = block(0), block(1)
    order = np.concatenate([index[0::2], index[1::2]])
    pick = np.eye(frame)[order]
    stack = np.stack([even, odd, even.T, odd.T, pick, pick.T])
    return stack.astype(np.float32).astype(ml_dtypes.bfloat16)


def halo_kernel(
    sample, right_out, below_out, corner_out,
    right_in, below_in, corner_in, edge, edge_below, edge_corner, send, recv,
    *, n_row, n_col,
):
    bf16 = jnp.bfloat16
    frame = right_out.shape[-1]
    row, col = lax.axis_index("row"), lax.axis_index("col")
    left = (row, lax.rem(col + n_col - 1, n_col))
    right = (row, lax.rem(col + 1, n_col))
    up = (lax.rem(row + n_row - 1, n_row), col)
    down = (lax.rem(row + 1, n_row), col)
    up_left = (up[0], left[1])
    down_right = (down[0], right[1])
    barrier = pltpu.get_barrier_semaphore()
    peers = (left, right, up, down, up_left, down_right)
    for peer in peers:
        pl.semaphore_signal(barrier, inc=1, device_id=peer, device_id_type=pl.DeviceIdType.MESH)
    edge[...] = sample[:, :, :frame].astype(bf16)
    edge_below[...] = sample[:, :frame, :].astype(bf16)
    edge_corner[...] = sample[:, :frame, :frame].astype(bf16)
    pl.semaphore_wait(barrier, len(peers))
    to_left, to_up = col > 0, row > 0
    has_right, has_below = col < n_col - 1, row < n_row - 1
    plan = [
        (edge, right_in, left, to_left, has_right, right_out),
        (edge_below, below_in, up, to_up, has_below, below_out),
        (edge_corner, corner_in, up_left, jnp.logical_and(to_left, to_up),
         jnp.logical_and(has_right, has_below), corner_out),
    ]
    copies = [
        pltpu.make_async_remote_copy(
            src_ref=src, dst_ref=dst, send_sem=send.at[i], recv_sem=recv.at[i],
            device_id=to, device_id_type=pl.DeviceIdType.MESH,
        )
        for i, (src, dst, to, _, _, _) in enumerate(plan)
    ]
    for one, item in zip(copies, plan):
        pl.when(item[3])(one.start)

    def finish(one, dst, has, out):
        @pl.when(has)
        def _():
            one.wait_recv()
            out[...] = dst[...]

        @pl.when(jnp.logical_not(has))
        def _():
            out[...] = jnp.zeros_like(out)

    for one, item in zip(copies, plan):
        finish(one, item[1], item[4], item[5])
    for one, item in zip(copies, plan):
        pl.when(item[3])(one.wait_send)


def gradient_kernel(
    offsets, counts, table, sample, right, below, corner, probe, amplitude,
    main_out, right_out, below_out, corner_out, probe_out,
    ext, acc, *pairs,
):
    rows, cols = sample.shape[1:]
    frame = probe.shape[-1]
    half = frame // 2
    own = cols // LANES
    wide = ext.shape[1]
    f32, bf16 = jnp.float32, jnp.bfloat16

    for c in range(2):
        for j in range(own):
            at = slice(j * LANES, (j + 1) * LANES)
            ext[c, j, :rows, :] = sample[c, :, at]
            ext[c, j, rows:, :] = below[c, :, at].astype(f32)
        for j in range(own, wide):
            at = slice((j - own) * LANES, (j - own + 1) * LANES)
            ext[c, j, :rows, :] = right[c, :, at].astype(f32)
            ext[c, j, rows:, :] = corner[c, :, at].astype(f32)
    acc[...] = jnp.zeros_like(acc)
    probe_out[...] = jnp.zeros_like(probe_out)

    def dot(a, b):
        return jnp.dot(a, b, preferred_element_type=f32)

    def visit(slot, turn):
        patch, xs, ys, zs, gs = (ref.at[turn] for ref in pairs)
        row_at = offsets[2 * slot]
        col_at = offsets[2 * slot + 1]
        panel = col_at // LANES
        lane_at = col_at % LANES
        back_by = lax.rem(LANES - lane_at, LANES)
        lane = lax.broadcasted_iota(jnp.int32, (CHUNK, LANES), 1)
        inside = lane < LANES - lane_at
        after = lane >= lane_at

        measured = dot(table[4], amplitude[slot]).astype(bf16)
        measured = dot(measured, table[5])

        def window(c, t):
            parts = [
                pltpu.roll(ext[c, panel + j, pl.ds(row_at + t, CHUNK), :], back_by, 1)
                for j in range(3)
            ]
            return [jnp.where(inside, parts[j], parts[j + 1]) for j in range(2)]

        for t in range(0, half, CHUNK):
            waves = []
            for h in range(2):
                u = h * half + t
                o_real, o_imag = window(0, u), window(1, u)
                wave = {}
                for j in range(2):
                    at = slice(j * LANES, (j + 1) * LANES)
                    patch[0, u : u + CHUNK, at] = o_real[j]
                    patch[1, u : u + CHUNK, at] = o_imag[j]
                    for m in range(2):
                        p_real = probe[m, 0, u : u + CHUNK, at]
                        p_imag = probe[m, 1, u : u + CHUNK, at]
                        wave[m, j, 0] = p_real * o_real[j] - p_imag * o_imag[j]
                        wave[m, j, 1] = p_real * o_imag[j] + p_imag * o_real[j]
                waves.append(wave)
            for m in range(2):
                for j in range(2):
                    at = slice(m * frame + j * LANES, m * frame + (j + 1) * LANES)
                    for c in range(2):
                        low, high = waves[0][m, j, c], waves[1][m, j, c]
                        to = slice(c * half + t, c * half + t + CHUNK)
                        xs[0, to, at] = (low + high).astype(bf16)
                        xs[1, to, at] = (low - high).astype(bf16)

        yield
        for p in range(2):
            product = dot(table[p], xs[p])
            for m in range(2):
                to = slice((2 * p + m) * half, (2 * p + m + 1) * half)
                for c in range(2):
                    value = product[c * half : (c + 1) * half, m * frame : (m + 1) * frame]
                    low, high = value[:, :half], value[:, half:]
                    at = slice(c * half, (c + 1) * half)
                    ys[0, to, at] = (low + high).astype(bf16)
                    ys[1, to, at] = (low - high).astype(bf16)

        yield
        for q in range(2):
            far = dot(ys[q], table[2 + q])
            for p in range(2):
                rows_of = [slice((2 * p + m) * half, (2 * p + m + 1) * half) for m in range(2)]
                fields = [[far[r, :half], far[r, half:]] for r in rows_of]
                intensity = sum(f[0] * f[0] + f[1] * f[1] for f in fields)
                level = measured[p * half : (p + 1) * half, q * half : (q + 1) * half]
                factor = 1.0 - level * lax.rsqrt(jnp.maximum(intensity, 0.0625))
                for m in range(2):
                    at = slice(m * frame + q * half, m * frame + (q + 1) * half)
                    for c in range(2):
                        zs[p, c * half : (c + 1) * half, at] = (fields[m][c] * factor).astype(bf16)

        yield
        from_even = dot(table[2], zs[0])
        from_odd = dot(table[3], zs[1])
        for h, back in enumerate((from_even + from_odd, from_even - from_odd)):
            for m in range(2):
                to = slice((2 * h + m) * half, (2 * h + m + 1) * half)
                for q in range(2):
                    at = slice(m * frame + q * half, m * frame + (q + 1) * half)
                    for c in range(2):
                        gs[q, to, c * half : (c + 1) * half] = back[
                            c * half : (c + 1) * half, at
                        ].astype(bf16)

        yield
        grad_even = dot(gs[0], table[0])
        grad_odd = dot(gs[1], table[1])
        for t in range(0, frame, CHUNK):
            h, u = divmod(t, half)
            terms = [[None, None], [None, None]]
            for j in range(2):
                at = slice(j * LANES, (j + 1) * LANES)
                here = slice(t, t + CHUNK)
                o_real, o_imag = patch[0, here, at], patch[1, here, at]
                for m in range(2):
                    of = slice((2 * h + m) * half + u, (2 * h + m) * half + u + CHUNK)
                    g = []
                    for c in range(2):
                        e = grad_even[of, c * half : (c + 1) * half]
                        o = grad_odd[of, c * half : (c + 1) * half]
                        g.append(e + o if j == 0 else e - o)
                    p_real, p_imag = probe[m, 0, here, at], probe[m, 1, here, at]
                    add_real = p_real * g[0] + p_imag * g[1]
                    add_imag = p_real * g[1] - p_imag * g[0]
                    terms[0][j] = add_real if m == 0 else terms[0][j] + add_real
                    terms[1][j] = add_imag if m == 0 else terms[1][j] + add_imag
                    probe_out[m, 0, here, at] += o_real * g[0] + o_imag * g[1]
                    probe_out[m, 1, here, at] += o_real * g[1] - o_imag * g[0]
            for c in range(2):
                first = pltpu.roll(terms[c][0], lane_at, 1)
                second = pltpu.roll(terms[c][1], lane_at, 1)
                spread = (
                    jnp.where(after, first, 0.0),
                    jnp.where(after, second, first),
                    jnp.where(after, 0.0, second),
                )
                for j in range(3):
                    acc[c, panel + j, pl.ds(row_at + t, CHUNK), :] += spread[j]
        yield

    def both(pair, carry):
        first, second = visit(2 * pair, 0), visit(2 * pair + 1, 1)
        next(first)
        for _ in range(4):
            next(first)
            next(second)
        next(second)
        return carry

    live = counts[0]
    lax.fori_loop(0, live // 2, both, 0)

    @pl.when(live % 2 == 1)
    def _():
        for _ in visit(live - 1, 0):
            pass

    for c in range(2):
        for j in range(own):
            at = slice(j * LANES, (j + 1) * LANES)
            main_out[c, :, at] = acc[c, j, :rows, :]
            below_out[c, :, at] = acc[c, j, rows:, :].astype(bf16)
        for j in range(own, wide):
            at = slice((j - own) * LANES, (j - own + 1) * LANES)
            right_out[c, :, at] = acc[c, j, :rows, :].astype(bf16)
            corner_out[c, :, at] = acc[c, j, rows:, :].astype(bf16)


def exchange_kernel(
    sample, main, right_grad, below_grad, corner_grad, probe, probe_grad,
    sample_out, probe_out,
    from_left, from_above, from_both, parts, col_buf, row_buf, col_sum, row_sum, gathered, whole,
    halo_send, halo_recv, col_send, col_recv, row_send, row_recv,
    row_send2, row_recv2, col_send2, col_recv2,
    *, n_row, n_col, rate,
):
    f32, bf16 = jnp.float32, jnp.bfloat16
    frame = probe.shape[-1]
    row, col = lax.axis_index("row"), lax.axis_index("col")
    col_chunk = parts.shape[0] // n_col
    row_chunk = col_chunk // n_row

    def on_row(k):
        return (lax.rem(row + k, n_row), col)

    def on_col(k):
        return (row, lax.rem(col + k, n_col))

    def copy(src, dst, send, recv, to):
        return pltpu.make_async_remote_copy(
            src_ref=src, dst_ref=dst, send_sem=send, recv_sem=recv,
            device_id=to, device_id_type=pl.DeviceIdType.MESH,
        )

    barrier = pltpu.get_barrier_semaphore()
    down_right = (lax.rem(row + 1, n_row), lax.rem(col + 1, n_col))
    up_left = (lax.rem(row + n_row - 1, n_row), lax.rem(col + n_col - 1, n_col))
    peers = [on_row(k) for k in range(1, n_row)] + [on_col(k) for k in range(1, n_col)]
    peers += [down_right, up_left]
    for peer in peers:
        pl.semaphore_signal(barrier, inc=1, device_id=peer, device_id_type=pl.DeviceIdType.MESH)

    panels = frame // LANES
    blocks = [(m, c, j) for m in range(2) for c in range(2) for j in range(panels)]
    for b, (m, c, j) in enumerate(blocks):
        value = probe_grad[m, c, :, j * LANES : (j + 1) * LANES]
        parts[b * frame : (b + 1) * frame, :] = value.astype(bf16)
    pl.semaphore_wait(barrier, len(peers))

    def rows_of(index, size):
        return pl.ds(pl.multiple_of(index * size, 16), size)

    scatter = [
        copy(
            parts.at[rows_of(lax.rem(col + k, n_col), col_chunk)], col_buf.at[k],
            col_send.at[k], col_recv.at[k], on_col(k),
        )
        for k in range(1, n_col)
    ]
    for one in scatter:
        one.start()

    gives_right, gives_below = col < n_col - 1, row < n_row - 1
    has_left, has_above = col > 0, row > 0
    halos = [
        (copy(right_grad, from_left, halo_send.at[0], halo_recv.at[0], on_col(1)),
         gives_right, has_left),
        (copy(below_grad.at[0], from_above.at[0], halo_send.at[1], halo_recv.at[1], on_row(1)),
         gives_below, has_above),
        (copy(below_grad.at[1], from_above.at[1], halo_send.at[3], halo_recv.at[3], on_row(1)),
         gives_below, has_above),
        (copy(corner_grad, from_both, halo_send.at[2], halo_recv.at[2], down_right),
         jnp.logical_and(gives_right, gives_below), jnp.logical_and(has_left, has_above)),
    ]
    pl.when(halos[1][1])(halos[1][0].start)

    for one in scatter:
        one.wait_recv()
    total = parts[rows_of(col, col_chunk), :].astype(f32)
    for k in range(1, n_col):
        total = total + col_buf[k].astype(f32)
    col_sum[...] = total
    reduce_rows = [
        copy(
            col_sum.at[rows_of(lax.rem(row + k, n_row), row_chunk)], row_buf.at[k],
            row_send.at[k], row_recv.at[k], on_row(k),
        )
        for k in range(1, n_row)
    ]
    for one in reduce_rows:
        one.start()
    pl.when(halos[0][1])(halos[0][0].start)

    power = probe[0, 0] ** 2 + probe[0, 1] ** 2 + (probe[1, 0] ** 2 + probe[1, 1] ** 2)
    scale = 1.0 / (jnp.max(power, keepdims=True) + 1e-06)
    for c in range(2):
        sample_out[c] = sample[c] - main[c] * scale

    for one in reduce_rows:
        one.wait_recv()
    total = col_sum[rows_of(row, row_chunk), :]
    for k in range(1, n_row):
        total = total + row_buf[k]
    row_sum[...] = total.astype(bf16)
    gather_rows = [
        copy(
            row_sum, gathered.at[rows_of(row, row_chunk)],
            row_send2.at[k], row_recv2.at[k], on_row(k),
        )
        for k in range(1, n_row)
    ]
    for one in gather_rows:
        one.start()
    gathered[rows_of(row, row_chunk), :] = row_sum[...]
    for one in gather_rows:
        one.wait_recv()
    for one, gives, _ in halos[2:]:
        pl.when(gives)(one.start)
    gather_cols = [
        copy(
            gathered, whole.at[rows_of(col, col_chunk)],
            col_send2.at[k], col_recv2.at[k], on_col(k),
        )
        for k in range(1, n_col)
    ]
    for one in gather_cols:
        one.start()
    whole[rows_of(col, col_chunk), :] = gathered[...]

    def take(halo, src, parts_of):
        one, _, has = halo
        rows, cols = src.shape[1:]

        @pl.when(has)
        def _():
            one.wait_recv()
            for c in parts_of:
                sample_out[c, :rows, :cols] -= src[c].astype(f32) * scale

    take(halos[1], from_above, (0,))
    take(halos[0], from_left, (0, 1))
    take(halos[2], from_above, (1,))
    take(halos[3], from_both, (0, 1))

    for one in gather_cols:
        one.wait_recv()
    for b, (m, c, j) in enumerate(blocks):
        at = slice(j * LANES, (j + 1) * LANES)
        summed = whole[b * frame : (b + 1) * frame, :].astype(f32)
        probe_out[m, c, :, at] = probe[m, c, :, at] - rate * summed
    for one in scatter + reduce_rows + gather_rows + gather_cols:
        one.wait_send()
    for one, gives, _ in halos:
        pl.when(gives)(one.wait_send)


def shards(sample, probe_modes, amplitude, offsets, counts):
    frame = probe_modes.shape[-1]
    rows, cols = sample.shape[1:]
    slots = amplitude.shape[2]
    f32, bf16 = jnp.float32, jnp.bfloat16
    panels = (cols + frame) // LANES
    shape = jax.ShapeDtypeStruct
    vmem = pl.BlockSpec(memory_space=pltpu.VMEM)
    smem = pl.BlockSpec(memory_space=pltpu.SMEM)
    n_row, n_col = lax.axis_size("row"), lax.axis_size("col")
    dma = pltpu.SemaphoreType.DMA
    halo_shapes = ((2, rows, frame), (2, frame, cols), (2, frame, frame))
    right, below, corner = pl.pallas_call(
        functools.partial(halo_kernel, n_row=n_row, n_col=n_col),
        out_shape=tuple(shape(h, bf16) for h in halo_shapes),
        in_specs=[vmem],
        out_specs=(vmem,) * 3,
        scratch_shapes=[pltpu.VMEM(h, bf16) for h in halo_shapes * 2] + [dma((3,)), dma((3,))],
        compiler_params=pltpu.CompilerParams(
            collective_id=1, has_side_effects=True, vmem_limit_bytes=32 * 1024 * 1024
        ),
    )(sample)
    main, right_grad, below_grad, corner_grad, probe_grad = pl.pallas_call(
        gradient_kernel,
        out_shape=(
            shape((2, rows, cols), f32),
            shape((2, rows, frame), bf16),
            shape((2, frame, cols), bf16),
            shape((2, frame, frame), bf16),
            shape(probe_modes.shape, f32),
        ),
        in_specs=[smem, smem] + [vmem] * 7,
        out_specs=(vmem,) * 5,
        scratch_shapes=[
            pltpu.VMEM((2, panels, rows + frame, LANES), f32),
            pltpu.VMEM((2, panels, rows + frame, LANES), f32),
            pltpu.VMEM((2, 2, frame, frame), f32),
            pltpu.VMEM((2, 2, frame, 2 * frame), bf16),
            pltpu.VMEM((2, 2, 2 * frame, frame), bf16),
            pltpu.VMEM((2, 2, frame, 2 * frame), bf16),
            pltpu.VMEM((2, 2, 2 * frame, frame), bf16),
        ],
        compiler_params=pltpu.CompilerParams(vmem_limit_bytes=48 * 1024 * 1024),
    )(
        offsets.reshape(-1), counts.reshape(-1), jnp.asarray(tables(frame)), sample,
        right, below, corner, probe_modes, amplitude.reshape(slots, frame, frame),
    )
    lines = probe_modes.size // LANES
    col_chunk = lines // n_col
    row_chunk = col_chunk // n_row
    return pl.pallas_call(
        functools.partial(
            exchange_kernel, n_row=n_row, n_col=n_col, rate=1.0 / math.sqrt(n_row * n_col * slots)
        ),
        out_shape=(shape(sample.shape, f32), shape(probe_modes.shape, f32)),
        in_specs=[vmem] * 7,
        out_specs=(vmem,) * 2,
        scratch_shapes=[
            pltpu.VMEM((2, rows, frame), bf16),
            pltpu.VMEM((2, frame, cols), bf16),
            pltpu.VMEM((2, frame, frame), bf16),
            pltpu.VMEM((lines, LANES), bf16),
            pltpu.VMEM((n_col, col_chunk, LANES), bf16),
            pltpu.VMEM((n_row, row_chunk, LANES), f32),
            pltpu.VMEM((col_chunk, LANES), f32),
            pltpu.VMEM((row_chunk, LANES), bf16),
            pltpu.VMEM((col_chunk, LANES), bf16),
            pltpu.VMEM((lines, LANES), bf16),
            dma((4,)), dma((4,)),
            dma((n_col,)), dma((n_col,)), dma((n_row,)), dma((n_row,)),
            dma((n_row,)), dma((n_row,)), dma((n_col,)), dma((n_col,)),
        ],
        compiler_params=pltpu.CompilerParams(
            collective_id=0, has_side_effects=True, vmem_limit_bytes=48 * 1024 * 1024
        ),
    )(sample, main, right_grad, below_grad, corner_grad, probe_modes, probe_grad)


def solution(mesh):
    in_specs = (
        P(None, "row", "col"),
        P(),
        P("row", "col", None, None, None),
        P("row", "col", None, None),
        P("row", "col"),
    )
    out_specs = (P(None, "row", "col"), P())
    return jax.shard_map(shards, mesh=mesh, in_specs=in_specs, out_specs=out_specs, check_vma=False)
```

```python
import functools
import math

import jax
import jax.numpy as jnp
import ml_dtypes
import numpy as np
from jax import lax
from jax.experimental import pallas as pl
from jax.experimental.pallas import tpu as pltpu
from jax.sharding import PartitionSpec as P

LANES = 128
CHUNK = 16


def tables(frame):
    index = np.arange(frame)
    angle = 2.0 * math.pi / frame * ((index[:, None] * index[None, :]) % frame)
    scale = 1.0 / math.sqrt(frame)
    w_real, w_imag = np.cos(angle) * scale, -np.sin(angle) * scale

    def block(first):
        real, imag = w_real[first::2, : frame // 2], w_imag[first::2, : frame // 2]
        return np.block([[real, -imag], [imag, real]])

    even, odd = block(0), block(1)
    order = np.concatenate([index[0::2], index[1::2]])
    pick = np.eye(frame)[order]
    stack = np.stack([even, odd, even.T, odd.T, pick, pick.T])
    return stack.astype(np.float32).astype(ml_dtypes.bfloat16)


def halo_kernel(
    sample, right_out, below_out, corner_out,
    right_in, below_in, corner_in, edge, edge_below, edge_corner, send, recv,
    *, n_row, n_col,
):
    bf16 = jnp.bfloat16
    frame = right_out.shape[-1]
    row, col = lax.axis_index("row"), lax.axis_index("col")
    left = (row, lax.rem(col + n_col - 1, n_col))
    right = (row, lax.rem(col + 1, n_col))
    up = (lax.rem(row + n_row - 1, n_row), col)
    down = (lax.rem(row + 1, n_row), col)
    up_left = (up[0], left[1])
    down_right = (down[0], right[1])
    barrier = pltpu.get_barrier_semaphore()
    peers = (left, right, up, down, up_left, down_right)
    for peer in peers:
        pl.semaphore_signal(barrier, inc=1, device_id=peer, device_id_type=pl.DeviceIdType.MESH)
    edge[...] = sample[:, :, :frame].astype(bf16)
    edge_below[...] = sample[:, :frame, :].astype(bf16)
    edge_corner[...] = sample[:, :frame, :frame].astype(bf16)
    pl.semaphore_wait(barrier, len(peers))
    to_left, to_up = col > 0, row > 0
    has_right, has_below = col < n_col - 1, row < n_row - 1
    plan = [
        (edge, right_in, left, to_left, has_right, right_out),
        (edge_below, below_in, up, to_up, has_below, below_out),
        (edge_corner, corner_in, up_left, jnp.logical_and(to_left, to_up),
         jnp.logical_and(has_right, has_below), corner_out),
    ]
    copies = [
        pltpu.make_async_remote_copy(
            src_ref=src, dst_ref=dst, send_sem=send.at[i], recv_sem=recv.at[i],
            device_id=to, device_id_type=pl.DeviceIdType.MESH,
        )
        for i, (src, dst, to, _, _, _) in enumerate(plan)
    ]
    for one, item in zip(copies, plan):
        pl.when(item[3])(one.start)

    def finish(one, dst, has, out):
        @pl.when(has)
        def _():
            one.wait_recv()
            out[...] = dst[...]

        @pl.when(jnp.logical_not(has))
        def _():
            out[...] = jnp.zeros_like(out)

    for one, item in zip(copies, plan):
        finish(one, item[1], item[4], item[5])
    for one, item in zip(copies, plan):
        pl.when(item[3])(one.wait_send)


def gradient_kernel(
    offsets, counts, table, sample, right, below, corner, probe, amplitude,
    main_out, right_out, below_out, corner_out, probe_out,
    ext, acc, *pairs,
):
    rows, cols = sample.shape[1:]
    frame = probe.shape[-1]
    half = frame // 2
    own = cols // LANES
    wide = ext.shape[1]
    f32, bf16 = jnp.float32, jnp.bfloat16

    for c in range(2):
        for j in range(own):
            at = slice(j * LANES, (j + 1) * LANES)
            ext[c, j, :rows, :] = sample[c, :, at]
            ext[c, j, rows:, :] = below[c, :, at].astype(f32)
        for j in range(own, wide):
            at = slice((j - own) * LANES, (j - own + 1) * LANES)
            ext[c, j, :rows, :] = right[c, :, at].astype(f32)
            ext[c, j, rows:, :] = corner[c, :, at].astype(f32)
    acc[...] = jnp.zeros_like(acc)
    probe_out[...] = jnp.zeros_like(probe_out)

    def dot(a, b):
        return jnp.dot(a, b, preferred_element_type=f32)

    def visit(slot, turn):
        patch, xs, ys, zs, gs = (ref.at[turn] for ref in pairs)
        row_at = offsets[2 * slot]
        col_at = offsets[2 * slot + 1]
        panel = col_at // LANES
        lane_at = col_at % LANES
        back_by = lax.rem(LANES - lane_at, LANES)
        lane = lax.broadcasted_iota(jnp.int32, (CHUNK, LANES), 1)
        inside = lane < LANES - lane_at
        after = lane >= lane_at

        measured = dot(table[4], amplitude[slot]).astype(bf16)
        measured = dot(measured, table[5])

        def window(c, t):
            parts = [
                pltpu.roll(ext[c, panel + j, pl.ds(row_at + t, CHUNK), :], back_by, 1)
                for j in range(3)
            ]
            return [jnp.where(inside, parts[j], parts[j + 1]) for j in range(2)]

        for t in range(0, half, CHUNK):
            waves = []
            for h in range(2):
                u = h * half + t
                o_real, o_imag = window(0, u), window(1, u)
                wave = {}
                for j in range(2):
                    at = slice(j * LANES, (j + 1) * LANES)
                    patch[0, u : u + CHUNK, at] = o_real[j]
                    patch[1, u : u + CHUNK, at] = o_imag[j]
                    for m in range(2):
                        p_real = probe[m, 0, u : u + CHUNK, at]
                        p_imag = probe[m, 1, u : u + CHUNK, at]
                        wave[m, j, 0] = p_real * o_real[j] - p_imag * o_imag[j]
                        wave[m, j, 1] = p_real * o_imag[j] + p_imag * o_real[j]
                waves.append(wave)
            for m in range(2):
                for j in range(2):
                    at = slice(m * frame + j * LANES, m * frame + (j + 1) * LANES)
                    for c in range(2):
                        low, high = waves[0][m, j, c], waves[1][m, j, c]
                        to = slice(c * half + t, c * half + t + CHUNK)
                        xs[0, to, at] = (low + high).astype(bf16)
                        xs[1, to, at] = (low - high).astype(bf16)

        yield
        for p in range(2):
            product = dot(table[p], xs[p])
            for m in range(2):
                to = slice((2 * p + m) * half, (2 * p + m + 1) * half)
                for c in range(2):
                    value = product[c * half : (c + 1) * half, m * frame : (m + 1) * frame]
                    low, high = value[:, :half], value[:, half:]
                    at = slice(c * half, (c + 1) * half)
                    ys[0, to, at] = (low + high).astype(bf16)
                    ys[1, to, at] = (low - high).astype(bf16)

        yield
        for q in range(2):
            far = dot(ys[q], table[2 + q])
            for p in range(2):
                rows_of = [slice((2 * p + m) * half, (2 * p + m + 1) * half) for m in range(2)]
                fields = [[far[r, :half], far[r, half:]] for r in rows_of]
                intensity = sum(f[0] * f[0] + f[1] * f[1] for f in fields)
                level = measured[p * half : (p + 1) * half, q * half : (q + 1) * half]
                factor = 1.0 - level * lax.rsqrt(jnp.maximum(intensity, 0.0625))
                for m in range(2):
                    at = slice(m * frame + q * half, m * frame + (q + 1) * half)
                    for c in range(2):
                        zs[p, c * half : (c + 1) * half, at] = (fields[m][c] * factor).astype(bf16)

        yield
        from_even = dot(table[2], zs[0])
        from_odd = dot(table[3], zs[1])
        for h, back in enumerate((from_even + from_odd, from_even - from_odd)):
            for m in range(2):
                to = slice((2 * h + m) * half, (2 * h + m + 1) * half)
                for q in range(2):
                    at = slice(m * frame + q * half, m * frame + (q + 1) * half)
                    for c in range(2):
                        gs[q, to, c * half : (c + 1) * half] = back[
                            c * half : (c + 1) * half, at
                        ].astype(bf16)

        yield
        grad_even = dot(gs[0], table[0])
        grad_odd = dot(gs[1], table[1])
        for t in range(0, frame, CHUNK):
            h, u = divmod(t, half)
            terms = [[None, None], [None, None]]
            for j in range(2):
                at = slice(j * LANES, (j + 1) * LANES)
                here = slice(t, t + CHUNK)
                o_real, o_imag = patch[0, here, at], patch[1, here, at]
                for m in range(2):
                    of = slice((2 * h + m) * half + u, (2 * h + m) * half + u + CHUNK)
                    g = []
                    for c in range(2):
                        e = grad_even[of, c * half : (c + 1) * half]
                        o = grad_odd[of, c * half : (c + 1) * half]
                        g.append(e + o if j == 0 else e - o)
                    p_real, p_imag = probe[m, 0, here, at], probe[m, 1, here, at]
                    add_real = p_real * g[0] + p_imag * g[1]
                    add_imag = p_real * g[1] - p_imag * g[0]
                    terms[0][j] = add_real if m == 0 else terms[0][j] + add_real
                    terms[1][j] = add_imag if m == 0 else terms[1][j] + add_imag
                    probe_out[m, 0, here, at] += o_real * g[0] + o_imag * g[1]
                    probe_out[m, 1, here, at] += o_real * g[1] - o_imag * g[0]
            for c in range(2):
                first = pltpu.roll(terms[c][0], lane_at, 1)
                second = pltpu.roll(terms[c][1], lane_at, 1)
                spread = (
                    jnp.where(after, first, 0.0),
                    jnp.where(after, second, first),
                    jnp.where(after, 0.0, second),
                )
                for j in range(3):
                    acc[c, panel + j, pl.ds(row_at + t, CHUNK), :] += spread[j]
        yield

    def both(pair, carry):
        first, second = visit(2 * pair, 0), visit(2 * pair + 1, 1)
        next(first)
        for _ in range(4):
            next(first)
            next(second)
        next(second)
        return carry

    live = counts[0]
    lax.fori_loop(0, live // 2, both, 0)

    @pl.when(live % 2 == 1)
    def _():
        for _ in visit(live - 1, 0):
            pass

    for c in range(2):
        for j in range(own):
            at = slice(j * LANES, (j + 1) * LANES)
            main_out[c, :, at] = acc[c, j, :rows, :]
            below_out[c, :, at] = acc[c, j, rows:, :].astype(bf16)
        for j in range(own, wide):
            at = slice((j - own) * LANES, (j - own + 1) * LANES)
            right_out[c, :, at] = acc[c, j, :rows, :].astype(bf16)
            corner_out[c, :, at] = acc[c, j, rows:, :].astype(bf16)


def exchange_kernel(
    sample, main, right_grad, below_grad, corner_grad, probe, probe_grad,
    sample_out, probe_out,
    from_left, from_above, from_both, parts, col_buf, row_buf, col_sum, row_sum, gathered, whole,
    halo_send, halo_recv, col_send, col_recv, row_send, row_recv,
    row_send2, row_recv2, col_send2, col_recv2,
    *, n_row, n_col, rate,
):
    f32, bf16 = jnp.float32, jnp.bfloat16
    frame = probe.shape[-1]
    row, col = lax.axis_index("row"), lax.axis_index("col")
    col_chunk = parts.shape[0] // n_col
    row_chunk = col_chunk // n_row

    def on_row(k):
        return (lax.rem(row + k, n_row), col)

    def on_col(k):
        return (row, lax.rem(col + k, n_col))

    def copy(src, dst, send, recv, to):
        return pltpu.make_async_remote_copy(
            src_ref=src, dst_ref=dst, send_sem=send, recv_sem=recv,
            device_id=to, device_id_type=pl.DeviceIdType.MESH,
        )

    barrier = pltpu.get_barrier_semaphore()
    down_right = (lax.rem(row + 1, n_row), lax.rem(col + 1, n_col))
    up_left = (lax.rem(row + n_row - 1, n_row), lax.rem(col + n_col - 1, n_col))
    peers = [on_row(k) for k in range(1, n_row)] + [on_col(k) for k in range(1, n_col)]
    peers += [down_right, up_left]
    for peer in peers:
        pl.semaphore_signal(barrier, inc=1, device_id=peer, device_id_type=pl.DeviceIdType.MESH)

    panels = frame // LANES
    blocks = [(m, c, j) for m in range(2) for c in range(2) for j in range(panels)]
    for b, (m, c, j) in enumerate(blocks):
        value = probe_grad[m, c, :, j * LANES : (j + 1) * LANES]
        parts[b * frame : (b + 1) * frame, :] = value.astype(bf16)
    pl.semaphore_wait(barrier, len(peers))

    def rows_of(index, size):
        return pl.ds(pl.multiple_of(index * size, 16), size)

    scatter = [
        copy(
            parts.at[rows_of(lax.rem(col + k, n_col), col_chunk)], col_buf.at[k],
            col_send.at[k], col_recv.at[k], on_col(k),
        )
        for k in range(1, n_col)
    ]
    for one in scatter:
        one.start()

    gives_right, gives_below = col < n_col - 1, row < n_row - 1
    has_left, has_above = col > 0, row > 0
    halos = [
        (copy(right_grad, from_left, halo_send.at[0], halo_recv.at[0], on_col(1)),
         gives_right, has_left),
        (copy(below_grad.at[0], from_above.at[0], halo_send.at[1], halo_recv.at[1], on_row(1)),
         gives_below, has_above),
        (copy(below_grad.at[1], from_above.at[1], halo_send.at[3], halo_recv.at[3], on_row(1)),
         gives_below, has_above),
        (copy(corner_grad, from_both, halo_send.at[2], halo_recv.at[2], down_right),
         jnp.logical_and(gives_right, gives_below), jnp.logical_and(has_left, has_above)),
    ]
    pl.when(halos[1][1])(halos[1][0].start)

    for one in scatter:
        one.wait_recv()
    total = parts[rows_of(col, col_chunk), :].astype(f32)
    for k in range(1, n_col):
        total = total + col_buf[k].astype(f32)
    col_sum[...] = total
    reduce_rows = [
        copy(
            col_sum.at[rows_of(lax.rem(row + k, n_row), row_chunk)], row_buf.at[k],
            row_send.at[k], row_recv.at[k], on_row(k),
        )
        for k in range(1, n_row)
    ]
    for one in reduce_rows:
        one.start()
    pl.when(halos[0][1])(halos[0][0].start)

    power = probe[0, 0] ** 2 + probe[0, 1] ** 2 + (probe[1, 0] ** 2 + probe[1, 1] ** 2)
    scale = 1.0 / (jnp.max(power, keepdims=True) + 1e-06)
    for c in range(2):
        sample_out[c] = sample[c] - main[c] * scale

    for one in reduce_rows:
        one.wait_recv()
    total = col_sum[rows_of(row, row_chunk), :]
    for k in range(1, n_row):
        total = total + row_buf[k]
    row_sum[...] = total.astype(bf16)
    gather_rows = [
        copy(
            row_sum, gathered.at[rows_of(row, row_chunk)],
            row_send2.at[k], row_recv2.at[k], on_row(k),
        )
        for k in range(1, n_row)
    ]
    for one in gather_rows:
        one.start()
    gathered[rows_of(row, row_chunk), :] = row_sum[...]
    for one in gather_rows:
        one.wait_recv()
    gather_cols = [
        copy(
            gathered, whole.at[rows_of(col, col_chunk)],
            col_send2.at[k], col_recv2.at[k], on_col(k),
        )
        for k in range(1, n_col)
    ]
    for one in gather_cols:
        one.start()
    for one, gives, _ in halos[2:]:
        pl.when(gives)(one.start)
    whole[rows_of(col, col_chunk), :] = gathered[...]

    def take(halo, src, parts_of):
        one, _, has = halo
        rows, cols = src.shape[1:]

        @pl.when(has)
        def _():
            one.wait_recv()
            for c in parts_of:
                sample_out[c, :rows, :cols] -= src[c].astype(f32) * scale

    take(halos[1], from_above, (0,))
    take(halos[0], from_left, (0, 1))
    take(halos[2], from_above, (1,))
    take(halos[3], from_both, (0, 1))

    for one in gather_cols:
        one.wait_recv()
    for b, (m, c, j) in enumerate(blocks):
        at = slice(j * LANES, (j + 1) * LANES)
        summed = whole[b * frame : (b + 1) * frame, :].astype(f32)
        probe_out[m, c, :, at] = probe[m, c, :, at] - rate * summed
    for one in scatter + reduce_rows + gather_rows + gather_cols:
        one.wait_send()
    for one, gives, _ in halos:
        pl.when(gives)(one.wait_send)


def shards(sample, probe_modes, amplitude, offsets, counts):
    frame = probe_modes.shape[-1]
    rows, cols = sample.shape[1:]
    slots = amplitude.shape[2]
    f32, bf16 = jnp.float32, jnp.bfloat16
    panels = (cols + frame) // LANES
    shape = jax.ShapeDtypeStruct
    vmem = pl.BlockSpec(memory_space=pltpu.VMEM)
    smem = pl.BlockSpec(memory_space=pltpu.SMEM)
    n_row, n_col = lax.axis_size("row"), lax.axis_size("col")
    dma = pltpu.SemaphoreType.DMA
    halo_shapes = ((2, rows, frame), (2, frame, cols), (2, frame, frame))
    right, below, corner = pl.pallas_call(
        functools.partial(halo_kernel, n_row=n_row, n_col=n_col),
        out_shape=tuple(shape(h, bf16) for h in halo_shapes),
        in_specs=[vmem],
        out_specs=(vmem,) * 3,
        scratch_shapes=[pltpu.VMEM(h, bf16) for h in halo_shapes * 2] + [dma((3,)), dma((3,))],
        compiler_params=pltpu.CompilerParams(
            collective_id=1, has_side_effects=True, vmem_limit_bytes=32 * 1024 * 1024
        ),
    )(sample)
    main, right_grad, below_grad, corner_grad, probe_grad = pl.pallas_call(
        gradient_kernel,
        out_shape=(
            shape((2, rows, cols), f32),
            shape((2, rows, frame), bf16),
            shape((2, frame, cols), bf16),
            shape((2, frame, frame), bf16),
            shape(probe_modes.shape, f32),
        ),
        in_specs=[smem, smem] + [vmem] * 7,
        out_specs=(vmem,) * 5,
        scratch_shapes=[
            pltpu.VMEM((2, panels, rows + frame, LANES), f32),
            pltpu.VMEM((2, panels, rows + frame, LANES), f32),
            pltpu.VMEM((2, 2, frame, frame), f32),
            pltpu.VMEM((2, 2, frame, 2 * frame), bf16),
            pltpu.VMEM((2, 2, 2 * frame, frame), bf16),
            pltpu.VMEM((2, 2, frame, 2 * frame), bf16),
            pltpu.VMEM((2, 2, 2 * frame, frame), bf16),
        ],
        compiler_params=pltpu.CompilerParams(vmem_limit_bytes=48 * 1024 * 1024),
    )(
        offsets.reshape(-1), counts.reshape(-1), jnp.asarray(tables(frame)), sample,
        right, below, corner, probe_modes, amplitude.reshape(slots, frame, frame),
    )
    lines = probe_modes.size // LANES
    col_chunk = lines // n_col
    row_chunk = col_chunk // n_row
    return pl.pallas_call(
        functools.partial(
            exchange_kernel, n_row=n_row, n_col=n_col, rate=1.0 / math.sqrt(n_row * n_col * slots)
        ),
        out_shape=(shape(sample.shape, f32), shape(probe_modes.shape, f32)),
        in_specs=[vmem] * 7,
        out_specs=(vmem,) * 2,
        scratch_shapes=[
            pltpu.VMEM((2, rows, frame), bf16),
            pltpu.VMEM((2, frame, cols), bf16),
            pltpu.VMEM((2, frame, frame), bf16),
            pltpu.VMEM((lines, LANES), bf16),
            pltpu.VMEM((n_col, col_chunk, LANES), bf16),
            pltpu.VMEM((n_row, row_chunk, LANES), f32),
            pltpu.VMEM((col_chunk, LANES), f32),
            pltpu.VMEM((row_chunk, LANES), bf16),
            pltpu.VMEM((col_chunk, LANES), bf16),
            pltpu.VMEM((lines, LANES), bf16),
            dma((4,)), dma((4,)),
            dma((n_col,)), dma((n_col,)), dma((n_row,)), dma((n_row,)),
            dma((n_row,)), dma((n_row,)), dma((n_col,)), dma((n_col,)),
        ],
        compiler_params=pltpu.CompilerParams(
            collective_id=0, has_side_effects=True, vmem_limit_bytes=48 * 1024 * 1024
        ),
    )(sample, main, right_grad, below_grad, corner_grad, probe_modes, probe_grad)


def solution(mesh):
    in_specs = (
        P(None, "row", "col"),
        P(),
        P("row", "col", None, None, None),
        P("row", "col", None, None),
        P("row", "col"),
    )
    out_specs = (P(None, "row", "col"), P())
    return jax.shard_map(shards, mesh=mesh, in_specs=in_specs, out_specs=out_specs, check_vma=False)
```
